512 devices in a mesh: row: 32 (over z, core), col: 16 (over y, x).
Axes of the slice: x: 4, y: 4, z: 16, core: 2. Of those that a mesh axis runs over, the one named last changes fastest.
Arguments:
- pred_feat: bfloat16 [327680, 64], P('row'), may hold values from -6 to 6
- true_feat: bfloat16 [262144, 64], P('col'), may hold values from -6 to 6
- neighbors: int32 [2560, 16, 12], P('row', 'col'), may hold values from 0 to 127, as said below
- counts: int32 [2560, 16], P('row'), may hold values from 0 to 12, as said below
Outputs:
- pred_potential: float32 [327680], P('row')
- true_potential: float32 [262144], P('col')
The draws below stay inside these ranges and needn't reach their ends.
Inputs may be any that keep to these rules, and one draw needn't show every extreme that they name: neighbors[b, s, k] indexes a block among the 128 ground-truth blocks of column shard s; entries at k >= counts[b, s] are ignored; the live entries of one list are distinct; every ground-truth block is named by some live entry. Each predicted block b has a first column shard h with counts[b, h] >= 1, may have live entries in shard h + 1 modulo 16, and has none in any other shard; of the blocks of one index of row exactly 80 / 16 have each column shard as their first, so at most 2 * 80 / 16 blocks of one index of row have live entries in one column shard.
All inputs are finite; a program needn't handle non-finite values.
Results may differ from the reference program's by a relative error of at most 0.0003.
Values sent between devices are 32-bit elements; how exact they have to be, the bound alone decides.
A program may use at most 64 MiB of HBM per device.

```python
import math
import jax
import jax.numpy as jnp
from jax import lax

F = 64
BLOCK = 128
KMAX = 12
ITERS = 3
RB_DEV = 80
CB_DEV = 128
ROW_BLOCKS = 2560
PRED_POINTS = 327680
TRUE_POINTS = 262144
N_ROW = 32
N_COL = 16


def local_pattern(key):
    keys = jax.random.split(jax.random.fold_in(key, 7), 6)
    perms = jax.vmap(lambda k: jax.random.permutation(k, RB_DEV))(jax.random.split(keys[0], N_ROW)).astype(jnp.int32)
    rows = jnp.arange(N_ROW, dtype=jnp.int32)[:, None]
    rotate = jax.random.randint(keys[1], (N_ROW, 1), 0, N_COL).astype(jnp.int32)
    home = (perms % N_COL + rotate) % N_COL
    group = rows * (RB_DEV // N_COL) + perms // N_COL
    offsets = jax.random.randint(keys[2], (N_COL,), 0, CB_DEV).astype(jnp.int32)
    home_start = (group + jnp.take(offsets, home)) % CB_DEV
    home_count = jax.random.randint(keys[3], (N_ROW, RB_DEV), 1, KMAX + 1).astype(jnp.int32)
    home_count = jnp.where((rows == 0) & (perms == 0), KMAX, home_count)
    spill_start = jax.random.randint(keys[4], (N_ROW, RB_DEV), 0, CB_DEV).astype(jnp.int32)
    spill_count = jnp.clip(jax.random.randint(keys[5], (N_ROW, RB_DEV), -(KMAX // 2), KMAX + 1), 0, KMAX).astype(jnp.int32)
    spill_count = jnp.where(rows == 0, jnp.maximum(spill_count, 1), spill_count)
    shards = jnp.arange(N_COL, dtype=jnp.int32)[None, None, :]
    is_home = shards == home[:, :, None]
    is_spill = shards == ((home + 1) % N_COL)[:, :, None]
    sizes = jnp.where(is_home, home_count[:, :, None], jnp.where(is_spill, spill_count[:, :, None], 0))
    starts = jnp.where(is_home, home_start[:, :, None], spill_start[:, :, None])
    slots = jnp.arange(KMAX, dtype=jnp.int32)
    ids = (starts[:, :, :, None] + slots[None, None, None, :]) % CB_DEV
    return (ids.reshape(ROW_BLOCKS, N_COL, KMAX).astype(jnp.int32), sizes.reshape(ROW_BLOCKS, N_COL).astype(jnp.int32))


def draw_neighbors(key, part):
    return local_pattern(key)[0]


def draw_counts(key, part):
    return local_pattern(key)[1]


def levels(key, shape, cuts, smallest, top_value):
    level, own = 1.0, jax.random.fold_in(key, 6)
    for dim, blocks in cuts:
        steps = jnp.exp(jax.random.uniform(jax.random.fold_in(own, dim), (blocks,), jnp.float32, smallest / len(cuts), top_value / len(cuts)))
        level = level * jnp.repeat(steps, shape[dim] // blocks).reshape([-1 if axis == dim else 1 for axis in range(len(shape))])
    return level


def noise(own_key, dims, spread, limit, cuts=(), held_as=jnp.bfloat16):
    drawn = spread * jax.random.normal(own_key, dims, jnp.float32)
    if cuts:
        drawn = drawn * levels(own_key, dims, cuts, -0.22, 0.18)
    return jnp.clip(drawn, -limit, limit).astype(held_as)


def setup_inputs(seed: int = 0) -> dict:
    key_list = jax.random.split(jax.random.key(seed), 5)
    pred_feat = noise(key_list[0], (PRED_POINTS, F), 1.0, 6.0, ((0, 32),))
    true_feat = noise(key_list[1], (TRUE_POINTS, F), 1.0, 6.0, ((0, 16),))
    neighbors = draw_neighbors(jax.random.fold_in(key_list[4], 71), 0)
    counts = draw_counts(jax.random.fold_in(key_list[4], 71), 0)
    return {"pred_feat": pred_feat, "true_feat": true_feat, "neighbors": neighbors, "counts": counts}


EPSILON = 0.02
NEGATIVE = -1e30


def pair_costs(pred_blocks, true_blocks, neighbor_ids):
    chosen = jnp.take(true_blocks, neighbor_ids, axis=0).astype(jnp.float32)
    pred_sq = jnp.sum(jnp.square(pred_blocks.astype(jnp.float32)), -1)
    true_sq = jnp.sum(jnp.square(true_blocks.astype(jnp.float32)), -1)
    cross = jnp.einsum("rpf,rkqf->rkpq", pred_blocks.astype(jnp.float32), chosen)
    near_sq = jnp.take(true_sq, neighbor_ids, axis=0)
    return (pred_sq[:, None, :, None] + near_sq[:, :, None, :] - 2.0 * cross) / F


def join_pairs(first, second):
    top = jnp.maximum(first[0], second[0])
    return (top, first[1] * jnp.exp(first[0] - top) + second[1] * jnp.exp(second[0] - top))


def compact(column, capacity):
    return jnp.argsort((column <= 0).astype(jnp.int32), stable=True)[:capacity].astype(jnp.int32)


def reference(pred_feat, true_feat, neighbors, counts):
    pred_all = pred_feat.reshape(N_ROW, RB_DEV, BLOCK, F)
    true_all = true_feat.reshape(N_COL, CB_DEV, BLOCK, F)
    lists = neighbors.reshape(N_ROW, RB_DEV, N_COL, KMAX)
    sizes = counts.reshape(N_ROW, RB_DEV, N_COL)
    log_pred = -math.log(PRED_POINTS)
    log_true = -math.log(TRUE_POINTS)
    capacity = 2 * RB_DEV // N_COL
    slots = jnp.arange(KMAX, dtype=jnp.int32)
    true_pot = jnp.zeros((N_COL, CB_DEV, BLOCK), jnp.float32)
    pred_pot = jnp.zeros((N_ROW, RB_DEV, BLOCK), jnp.float32)
    for step in range(ITERS):
        def row_shard(index):
            pred_blocks = pred_all[index]
            def over_cols(carry, items):
                true_blocks, all_ids, all_count, pot = items
                picked = compact(all_count, capacity)
                ids = jnp.take(all_ids, picked, axis=0)
                live_count = jnp.take(all_count, picked, axis=0)
                cost = pair_costs(jnp.take(pred_blocks, picked, axis=0), true_blocks, ids)
                live = (slots[None, :] < live_count[:, None])[:, :, None, None]
                near = jnp.take(pot, ids, axis=0)
                scores = jnp.where(live, (near[:, :, None, :] - cost) / EPSILON, NEGATIVE)
                top = jnp.max(scores, axis=(1, 3))
                total = jnp.sum(jnp.where(live, jnp.exp(scores - top[:, None, :, None]), 0.0), axis=(1, 3))
                full_top = jnp.full((RB_DEV, BLOCK), NEGATIVE, jnp.float32).at[picked].set(top)
                full_total = jnp.zeros((RB_DEV, BLOCK), jnp.float32).at[picked].set(total)
                return join_pairs(carry, (full_top, full_total)), None
            init = (jnp.full((RB_DEV, BLOCK), NEGATIVE, jnp.float32), jnp.zeros((RB_DEV, BLOCK), jnp.float32))
            items = (true_all, jnp.transpose(lists[index], (1, 0, 2)), jnp.transpose(sizes[index], (1, 0)), true_pot)
            (top, total), unused = lax.scan(over_cols, init, items)
            return EPSILON * (log_pred - top - jnp.log(total))
        pred_pot = lax.map(row_shard, jnp.arange(N_ROW, dtype=jnp.int32))

        def col_shard(index):
            true_blocks = true_all[index]
            owner_ids = jnp.arange(CB_DEV, dtype=jnp.int32)
            def over_rows(carry, items):
                pred_blocks, all_ids, all_count, all_pot = items
                picked = compact(all_count, capacity)
                ids = jnp.take(all_ids, picked, axis=0)
                live_count = jnp.take(all_count, picked, axis=0)
                pot = jnp.take(all_pot, picked, axis=0)
                cost = pair_costs(jnp.take(pred_blocks, picked, axis=0), true_blocks, ids)
                live_pair = slots[None, :] < live_count[:, None]
                live = live_pair[:, :, None, None]
                scores = jnp.where(live, (pot[:, None, :, None] - cost) / EPSILON, NEGATIVE)
                owner = ((ids[:, :, None] == owner_ids[None, None, :]) & live_pair[:, :, None]).astype(jnp.float32)
                pair_top = jnp.max(scores, axis=2)
                top = jnp.max(jnp.where(owner[:, :, :, None] > 0, pair_top[:, :, None, :], NEGATIVE), axis=(0, 1))
                chosen_top = jnp.take(top, ids, axis=0)
                part = jnp.sum(jnp.where(live, jnp.exp(scores - chosen_top[:, :, None, :]), 0.0), axis=2)
                total = jnp.einsum("rkc,rkq->cq", owner, part, precision=lax.Precision.HIGHEST)
                return join_pairs(carry, (top, total)), None
            init = (jnp.full((CB_DEV, BLOCK), NEGATIVE, jnp.float32), jnp.zeros((CB_DEV, BLOCK), jnp.float32))
            items = (pred_all, lists[:, :, index, :], sizes[:, :, index], pred_pot)
            (top, total), unused = lax.scan(over_rows, init, items)
            return EPSILON * (log_true - top - jnp.log(total))
        true_pot = lax.map(col_shard, jnp.arange(N_COL, dtype=jnp.int32))
    return pred_pot.reshape(-1), true_pot.reshape(-1)
```

```python
import functools
import math

import jax
import jax.numpy as jnp
from jax import lax
from jax.experimental import pallas as pl
from jax.experimental.pallas import tpu as pltpu
from jax.sharding import PartitionSpec as P

BLOCK = 128
ITERS = 3
EPSILON = 0.02
NEGATIVE = -1e30
TILE = 8
CORES = 2
LISTS = 16
PICK_LANE = 63
UNIT = 1.0 / (EPSILON * math.log(2.0))
MESH = pl.DeviceIdType.MESH
F32, BF16, I32 = jnp.float32, jnp.bfloat16, jnp.int32


def dot(a, b, b_axis):
    return lax.dot_general(a, b, (((1,), (b_axis,)), ((), ())), preferred_element_type=F32)


def iota(shape, axis):
    return lax.broadcasted_iota(I32, shape, axis)


def join(a, b):
    high, low = jnp.maximum(a, b), jnp.minimum(a, b)
    return high + jnp.log2(1.0 + jnp.exp2(low - high))


def tree(op, items):
    items = list(items)
    while len(items) > 1:
        items = [op(*items[i : i + 2]) if i + 1 < len(items) else items[i] for i in range(0, len(items), 2)]
    return items[0]


def top_and_total(items):
    top = tree(jnp.maximum, items)
    return top, tree(jnp.add, [jnp.exp2(item - top) for item in items])


def square_norms(block):
    wide = block.astype(F32)
    return jnp.sum(wide * wide, axis=0, keepdims=True)


def block_of(features, index):
    return features[:, pl.ds(pl.multiple_of(BLOCK * index, BLOCK), BLOCK)]


def slot_row(b, homes):
    return jnp.where(b < homes, b, b + (TILE - homes))


def prepare_kernel(
    ncol, homes, counts_ref, neighbors_ref, pred_hbm, true_hbm, table_ref, onehot, cost, pred_norm, true_norm,
    pred, true, table, load_sem,
):
    here = lax.axis_index("col")
    width, cblocks = true.shape[0], true_norm.shape[0]
    slots = 2 * homes
    loads = [
        pltpu.make_async_copy(true_hbm, true, load_sem.at[0]),
        pltpu.make_async_copy(pred_hbm, pred, load_sem.at[1]),
    ]
    for load in loads:
        load.start()
    counts = counts_ref[...].astype(F32)
    blocks, kmax = counts.shape[1], neighbors_ref.shape[0]
    to, frm = iota((ncol, ncol), 0), iota((ncol, ncol), 1)
    before = (frm == lax.rem(to + (ncol - 1), ncol)).astype(F32)
    home = ((counts > 0.5) & (dot(before, counts, 0) < 0.5)).astype(F32)
    upto = (iota((blocks, blocks), 0) <= iota((blocks, blocks), 1)).astype(F32)
    rank = dot(home, upto, 0) - 1.0
    shard = iota(home.shape, 0).astype(F32)
    place = jnp.sum(home * (TILE * shard + rank), axis=0, keepdims=True)
    slot = iota((2 * TILE, blocks), 0)
    owner = jnp.where(slot < TILE, here, lax.rem(here + (ncol - 1), ncol))
    wanted = (TILE * owner + lax.rem(slot, TILE)).astype(F32)
    chosen = (place == wanted).astype(F32)
    count = jnp.sum(jnp.where(iota(counts.shape, 0) == here, counts, 0.0), axis=0, keepdims=True)
    count = jnp.sum(chosen * count, axis=1, keepdims=True)
    pick = jnp.sum(chosen * iota(chosen.shape, 1).astype(F32), axis=1, keepdims=True)
    lane = iota((kmax, BLOCK), 1)
    repeat = ((lax.rem(lane, LISTS) == iota((kmax, BLOCK), 0)) & (lane < 3 * LISTS)).astype(F32)
    listed = dot(dot(chosen, neighbors_ref[:, 0, :].astype(F32), 1), repeat, 0)
    lane = iota(listed.shape, 1)
    live = lax.rem(lane, LISTS).astype(F32) < count
    found = jnp.where(lane == PICK_LANE, pick, jnp.where(live, listed, float(cblocks)))
    table_ref[0 : 2 * TILE, :] = found.astype(I32)
    table_ref[2 * TILE : 3 * TILE, :] = jnp.zeros((TILE, BLOCK), I32)
    table_ref[2 * TILE : 2 * TILE + 1, 0:blocks] = place.astype(I32)
    to_scalar = pltpu.make_async_copy(table_ref, table, load_sem.at[2])
    to_scalar.start()

    def match_blocks(b, carry):
        listed = table_ref[pl.ds(slot_row(b, homes), 1), 0 : 4 * LISTS]
        lane = iota((cblocks, 4 * LISTS), 1)
        match = ((iota((cblocks, 4 * LISTS), 0) == listed) & (lane < 3 * LISTS)).astype(F32)
        absent = 1.0 - jnp.sum(jnp.where(lane < LISTS, match, 0.0), axis=1, keepdims=True)
        onehot[b] = jnp.where(lane == 3 * LISTS, absent, match).astype(BF16)
        return carry

    lax.fori_loop(0, slots, match_blocks, 0)

    loads[0].wait()

    def norm_row(i, carry):
        true_norm[pl.ds(i, 1), :] = square_norms(block_of(true, i)) * (UNIT / width)
        return carry

    lax.fori_loop(0, cblocks, norm_row, 0, unroll=8)
    loads[1].wait()
    to_scalar.wait()
    pred_norm[...] = jnp.zeros((TILE, BLOCK), F32)
    for b in range(homes):
        pred_norm[b : b + 1, :] = square_norms(block_of(pred, table[b, PICK_LANE])) * (UNIT / width)

    def products(b, carry):
        at = slot_row(b, homes)
        mine = jnp.transpose(block_of(pred, table[at, PICK_LANE]))
        for k in range(neighbors_ref.shape[0]):
            other = block_of(true, jnp.minimum(table[at, k], cblocks - 1))
            cost[b * kmax + k] = dot(mine, other, 0) * (2.0 * UNIT / width)
        return carry

    lax.fori_loop(0, slots, products, 0)


def sinkhorn_kernel(
    sizes, table, onehot, cost, pred_norm, true_norm, pred_out, true_out,
    potential, columns, tops, sums, spread,
    part, parts, mate_out, mate_in, share, swap_out, swap_in, last_out, last_in,
    part_send, part_recv, mate_send, mate_recv, share_send, share_recv, swap_send, swap_recv,
    last_send, last_recv,
):
    nz, ncol, homes, kmax, log_a, log_b = sizes
    row, col = lax.axis_index("row"), lax.axis_index("col")
    z, core = row // CORES, lax.rem(row, CORES)
    slots = 2 * homes
    cblocks = true_norm.shape[0]
    right, left = lax.rem(col + 1, ncol), lax.rem(col + (ncol - 1), ncol)

    def far_first(i, n):
        return n // 2 + (1 - 2 * lax.rem(i, 2)) * ((i + 1) // 2)

    def along_z(d):
        return {"row": lax.rem(z + d, nz) * CORES + core}

    barrier = pltpu.get_barrier_semaphore()

    def greet_z(i, carry):
        pl.semaphore_signal(barrier, inc=1, device_id=along_z(i), device_id_type=MESH)
        return carry

    def greet_col(i, carry):
        pl.semaphore_signal(barrier, inc=1, device_id={"col": lax.rem(col + i, ncol)}, device_id_type=MESH)
        return carry

    lax.fori_loop(1, nz, greet_z, 0)
    lax.fori_loop(1, ncol, greet_col, 0)
    pl.semaphore_signal(barrier, inc=1, device_id={"row": z * CORES + (1 - core)}, device_id_type=MESH)

    for step in range(ITERS):
        potential[step, cblocks : cblocks + TILE, :] = jnp.full((TILE, BLOCK), NEGATIVE, F32)
    columns[...] = jnp.zeros((BLOCK, BLOCK), F32)

    def fill(b, carry):
        tops[b] = jnp.zeros((LISTS, BLOCK), F32)
        sums[b] = jnp.ones((LISTS, BLOCK), F32)
        return carry

    lax.fori_loop(0, slots, fill, 0)

    def share_copy(stage, d):
        return pltpu.make_async_remote_copy(
            src_ref=share.at[stage],
            dst_ref=potential.at[stage, pl.ds(TILE * z, TILE)],
            send_sem=share_send.at[stage, d],
            recv_sem=share_recv.at[stage, d],
            device_id=along_z(d),
            device_id_type=MESH,
        )

    def share_start(stage, value):
        share[stage] = value
        potential[stage, pl.ds(pl.multiple_of(TILE * z, TILE), TILE), :] = value

        def send(i, carry):
            share_copy(stage, far_first(i, nz)).start()
            return carry

        lax.fori_loop(0, nz - 1, send, 0)

    def share_wait(stage):
        def wait(i, carry):
            d = far_first(nz - 2 - i, nz)
            frm = lax.rem(z + (nz - d), nz)
            pltpu.make_async_remote_copy(
                src_ref=share.at[stage],
                dst_ref=potential.at[stage, pl.ds(TILE * frm, TILE)],
                send_sem=share_send.at[stage, d],
                recv_sem=share_recv.at[stage, d],
                device_id=along_z(d),
                device_id_type=MESH,
            ).wait()
            return carry

        lax.fori_loop(0, nz - 1, wait, 0)

    def block_of(features, index):
        return features[:, pl.ds(pl.multiple_of(BLOCK * index, BLOCK), BLOCK)]

    potential[0, 0:cblocks, :] = -true_norm[...]
    pl.semaphore_wait(barrier, nz + ncol - 1)

    def iteration(step, carry):
        def over_true(b, carry):
            at = slot_row(b, homes)
            near = [potential[step, pl.ds(table[at, k], 1), :] for k in range(kmax)]

            def rows(i, carry):
                here = pl.ds(pl.multiple_of(2 * TILE * i, 2 * TILE), 2 * TILE)
                top, total = top_and_total([cost[b * kmax + k, here, :] + near[k] for k in range(kmax)])
                high = jnp.max(top, axis=1, keepdims=True)
                total = jnp.sum(total * jnp.exp2(top - high), axis=1, keepdims=True)
                columns[here, :] = jnp.where(iota((2 * TILE, BLOCK), 1) == at, high + jnp.log2(total), columns[here, :])
                return carry

            lax.fori_loop(0, BLOCK // (2 * TILE), rows, 0, unroll=2)
            return carry

        lax.fori_loop(0, slots, over_true, 0)
        swap_out[step] = jnp.transpose(columns[...])[0 : 2 * TILE, :]

        def swap_copy(near):
            return pltpu.make_async_remote_copy(
                src_ref=swap_out.at[step, pl.ds(0 if near else TILE, TILE)],
                dst_ref=swap_in.at[step, pl.ds(TILE if near else 0, TILE)],
                send_sem=swap_send.at[step, int(near)],
                recv_sem=swap_recv.at[step, int(near)],
                device_id={"col": right if near else left},
                device_id_type=MESH,
            )

        for near in (True, False):
            swap_copy(near).start()
        for near in (True, False):
            swap_copy(near).wait()
        pred_rows = log_a - join(swap_out[step], swap_in[step])

        def last_copy(d, frm):
            return pltpu.make_async_remote_copy(
                src_ref=last_out,
                dst_ref=last_in.at[pl.ds(TILE * frm, TILE)],
                send_sem=last_send.at[d],
                recv_sem=last_recv.at[d],
                device_id={"col": lax.rem(col + d, ncol)},
                device_id_type=MESH,
            )

        @pl.when(step == ITERS - 1)
        def _():
            final = (pred_rows[0:TILE, :] + pred_norm[...]) * (1.0 / UNIT)
            last_out[...] = final
            last_in[pl.ds(pl.multiple_of(TILE * col, TILE), TILE), :] = final

            def send(i, carry):
                last_copy(far_first(i, ncol), col).start()
                return carry

            lax.fori_loop(0, ncol - 1, send, 0)

        columns[...] = jnp.transpose(jnp.concatenate([pred_rows, jnp.zeros((BLOCK - 2 * TILE, BLOCK), F32)], axis=0))

        def over_pred(b, carry):
            at = slot_row(b, homes)
            mine = []
            for i in range(BLOCK // TILE):
                held = columns[i * TILE : (i + 1) * TILE, :]
                picked = jnp.sum(jnp.where(iota((TILE, BLOCK), 1) == at, held, 0.0), axis=1, keepdims=True)
                mine.append(jnp.broadcast_to(picked, (TILE, BLOCK)))
            for k in range(kmax):
                top, total = top_and_total(
                    [cost[b * kmax + k, i * TILE : (i + 1) * TILE, :] + mine[i] for i in range(BLOCK // TILE)]
                )
                high = jnp.max(top, axis=0, keepdims=True)
                tops[b, k : k + 1, :] = high
                sums[b, k : k + 1, :] = jnp.sum(total * jnp.exp2(top - high), axis=0, keepdims=True)
            return carry

        lax.fori_loop(0, slots, over_pred, 0)

        def expand(b, carry):
            value = tops[b] + jnp.log2(sums[b])
            first = value.astype(BF16)
            rest = value - first.astype(F32)
            second = rest.astype(BF16)
            third = (rest - second.astype(F32)).astype(BF16)
            none = jnp.where(iota((LISTS, BLOCK), 0) == 0, NEGATIVE, 0.0).astype(BF16)
            spread[b] = dot(onehot[b], jnp.concatenate([first, second, third, none], axis=0), 0)
            return carry

        lax.fori_loop(0, slots, expand, 0)

        def gather(i, carry):
            here = pl.ds(pl.multiple_of(TILE * i, TILE), TILE)
            top, total = top_and_total([spread[b, here, :] for b in range(slots)])
            part[step, here, :] = top + jnp.log2(total)
            return carry

        lax.fori_loop(0, cblocks // TILE, gather, 0, unroll=2)

        def part_copy(d, to, frm):
            return pltpu.make_async_remote_copy(
                src_ref=part.at[step, pl.ds(TILE * to, TILE)],
                dst_ref=parts.at[step, pl.ds(TILE * frm, TILE)],
                send_sem=part_send.at[step, d],
                recv_sem=part_recv.at[step, d],
                device_id=along_z(d),
                device_id_type=MESH,
            )

        def part_start(i, carry):
            d = far_first(i, nz)
            part_copy(d, lax.rem(z + d, nz), z).start()
            return carry

        def part_wait(i, carry):
            d = far_first(nz - 2 - i, nz)
            part_copy(d, lax.rem(z + d, nz), lax.rem(z + (nz - d), nz)).wait()
            return carry

        lax.fori_loop(0, nz - 1, part_start, 0)
        own = pl.ds(pl.multiple_of(TILE * z, TILE), TILE)
        parts[step, own, :] = part[step, own, :]
        lax.fori_loop(0, nz - 1, part_wait, 0)
        top, total = top_and_total([parts[step, i * TILE : (i + 1) * TILE, :] for i in range(nz)])
        mate_out[step] = top + jnp.log2(total)
        mate = pltpu.make_async_remote_copy(
            src_ref=mate_out.at[step],
            dst_ref=mate_in.at[step],
            send_sem=mate_send.at[step],
            recv_sem=mate_recv.at[step],
            device_id={"row": z * CORES + (1 - core)},
            device_id_type=MESH,
        )
        mate.start()
        mate.wait()
        fresh = log_b - join(mate_out[step], mate_in[step])
        share_start(step + 1, jnp.where(step == ITERS - 1, (fresh + true_norm[own, :]) * (1.0 / UNIT), fresh))

        @pl.when(step == ITERS - 1)
        def _():
            def wait(i, carry):
                d = far_first(ncol - 2 - i, ncol)
                last_copy(d, lax.rem(col + (ncol - d), ncol)).wait()
                return carry

            lax.fori_loop(0, ncol - 1, wait, 0)

            def place(i, carry):
                pred_out[pl.ds(i, 1), :] = last_in[pl.ds(table[2 * TILE, i], 1), :]
                return carry

            lax.fori_loop(0, pred_out.shape[0], place, 0, unroll=8)

        share_wait(step + 1)
        return carry

    lax.fori_loop(0, ITERS, iteration, 0)
    true_out[...] = potential[ITERS, 0:cblocks, :]


def on_device(pred_feat, true_feat, neighbors, counts):
    width = pred_feat.shape[1]
    rblocks, cblocks = pred_feat.shape[0] // BLOCK, true_feat.shape[0] // BLOCK
    nrow, ncol = lax.axis_size("row"), lax.axis_size("col")
    nz, homes, kmax = nrow // CORES, rblocks // ncol, neighbors.shape[2]
    slots = 2 * homes
    log_a = -math.log2(pred_feat.shape[0] * nrow)
    log_b = -math.log2(true_feat.shape[0] * ncol)
    vmem = pl.BlockSpec(memory_space=pltpu.VMEM)
    anywhere = pl.BlockSpec(memory_space=pl.ANY)
    dma = pltpu.SemaphoreType.DMA
    ready = pl.pallas_call(
        functools.partial(prepare_kernel, ncol, homes),
        out_shape=(
            jax.ShapeDtypeStruct((3 * TILE, BLOCK), I32),
            jax.ShapeDtypeStruct((slots, cblocks, 4 * LISTS), BF16),
            jax.ShapeDtypeStruct((slots * kmax, BLOCK, BLOCK), F32),
            jax.ShapeDtypeStruct((TILE, BLOCK), F32),
            jax.ShapeDtypeStruct((cblocks, BLOCK), F32),
        ),
        in_specs=[vmem, vmem, anywhere, anywhere],
        out_specs=(vmem,) * 5,
        scratch_shapes=[
            pltpu.VMEM((width, rblocks * BLOCK), BF16),
            pltpu.VMEM((width, cblocks * BLOCK), BF16),
            pltpu.SMEM((3 * TILE, BLOCK), I32),
            dma((3,)),
        ],
        compiler_params=pltpu.CompilerParams(vmem_limit_bytes=24 * 2**20),
        name="prepare",
    )(counts.T, jnp.transpose(neighbors, (2, 1, 0)), pred_feat.T, true_feat.T)
    pred_pot, true_pot = pl.pallas_call(
        functools.partial(sinkhorn_kernel, (nz, ncol, homes, kmax, log_a, log_b)),
        out_shape=(
            jax.ShapeDtypeStruct((rblocks, BLOCK), F32),
            jax.ShapeDtypeStruct((cblocks, BLOCK), F32),
        ),
        in_specs=[
            pl.BlockSpec(memory_space=pltpu.SMEM),
            vmem,
            vmem,
            vmem,
            vmem,
        ],
        out_specs=(vmem, vmem),
        scratch_shapes=[
            pltpu.VMEM((ITERS + 1, cblocks + TILE, BLOCK), F32),
            pltpu.VMEM((BLOCK, BLOCK), F32),
            pltpu.VMEM((slots, LISTS, BLOCK), F32),
            pltpu.VMEM((slots, LISTS, BLOCK), F32),
            pltpu.VMEM((slots, cblocks, BLOCK), F32),
            pltpu.VMEM((ITERS, cblocks, BLOCK), F32),
            pltpu.VMEM((ITERS, cblocks, BLOCK), F32),
            pltpu.VMEM((ITERS, TILE, BLOCK), F32),
            pltpu.VMEM((ITERS, TILE, BLOCK), F32),
            pltpu.VMEM((ITERS + 1, TILE, BLOCK), F32),
            pltpu.VMEM((ITERS, 2 * TILE, BLOCK), F32),
            pltpu.VMEM((ITERS, 2 * TILE, BLOCK), F32),
            pltpu.VMEM((TILE, BLOCK), F32),
            pltpu.VMEM((TILE * ncol, BLOCK), F32),
            dma((ITERS, nz)),
            dma((ITERS, nz)),
            dma((ITERS,)),
            dma((ITERS,)),
            dma((ITERS + 1, nz)),
            dma((ITERS + 1, nz)),
            dma((ITERS, 2)),
            dma((ITERS, 2)),
            dma((ncol,)),
            dma((ncol,)),
        ],
        compiler_params=pltpu.CompilerParams(
            collective_id=0, has_side_effects=True, vmem_limit_bytes=24 * 2**20
        ),
        name="sinkhorn",
    )(*ready)
    return (pred_pot.reshape(-1), true_pot.reshape(-1))


def solution(mesh):
    in_specs = (P("row", None), P("col", None), P("row", "col", None), P("row", None))
    out_specs = (P("row"), P("col"))
    return jax.shard_map(
        on_device, mesh=mesh, in_specs=in_specs, out_specs=out_specs, check_vma=False
    )
```

```python
import functools
import math

import jax
import jax.numpy as jnp
from jax import lax
from jax.experimental import pallas as pl
from jax.experimental.pallas import tpu as pltpu
from jax.sharding import PartitionSpec as P

BLOCK = 128
ITERS = 3
EPSILON = 0.02
NEGATIVE = -1e30
TILE = 8
CORES = 2
ROWS = 16
OWNERS = 4
LISTS = 16
PICK_LANE = 63
UNIT = 1.0 / (EPSILON * math.log(2.0))
MESH = pl.DeviceIdType.MESH
F32, BF16, I32 = jnp.float32, jnp.bfloat16, jnp.int32


def dot(a, b, b_axis):
    return lax.dot_general(a, b, (((1,), (b_axis,)), ((), ())), preferred_element_type=F32)


def iota(shape, axis):
    return lax.broadcasted_iota(I32, shape, axis)


def join(a, b):
    high, low = jnp.maximum(a, b), jnp.minimum(a, b)
    return high + jnp.log2(1.0 + jnp.exp2(low - high))


def tree(op, items):
    items = list(items)
    while len(items) > 1:
        items = [op(*items[i : i + 2]) if i + 1 < len(items) else items[i] for i in range(0, len(items), 2)]
    return items[0]


def top_and_total(items):
    top = tree(jnp.maximum, items)
    return top, tree(jnp.add, [jnp.exp2(item - top) for item in items])


def square_norms(block):
    wide = block.astype(F32)
    return jnp.sum(wide * wide, axis=0, keepdims=True)


def block_of(features, index):
    return features[:, pl.ds(pl.multiple_of(BLOCK * index, BLOCK), BLOCK)]


def slot_row(b, homes):
    return jnp.where(b < homes, b, b + (TILE - homes))


def prepare_kernel(
    ncol, homes, counts_ref, neighbors_ref, pred_hbm, true_hbm, table_ref, onehot, cost, pred_norm, true_norm,
    pred, true, table, load_sem,
):
    here = lax.axis_index("col")
    width, cblocks = true.shape[0], true_norm.shape[0]
    slots = 2 * homes
    loads = [
        pltpu.make_async_copy(true_hbm, true, load_sem.at[0]),
        pltpu.make_async_copy(pred_hbm, pred, load_sem.at[1]),
    ]
    for load in loads:
        load.start()
    counts = counts_ref[...].astype(F32)
    blocks, kmax = counts.shape[1], neighbors_ref.shape[0]
    to, frm = iota((ncol, ncol), 0), iota((ncol, ncol), 1)
    before = (frm == lax.rem(to + (ncol - 1), ncol)).astype(F32)
    home = ((counts > 0.5) & (dot(before, counts, 0) < 0.5)).astype(F32)
    upto = (iota((blocks, blocks), 0) <= iota((blocks, blocks), 1)).astype(F32)
    rank = dot(home, upto, 0) - 1.0
    shard = iota(home.shape, 0).astype(F32)
    place = jnp.sum(home * (TILE * shard + rank), axis=0, keepdims=True)
    slot = iota((2 * TILE, blocks), 0)
    owner = jnp.where(slot < TILE, here, lax.rem(here + (ncol - 1), ncol))
    wanted = (TILE * owner + lax.rem(slot, TILE)).astype(F32)
    chosen = (place == wanted).astype(F32)
    count = jnp.sum(jnp.where(iota(counts.shape, 0) == here, counts, 0.0), axis=0, keepdims=True)
    count = jnp.sum(chosen * count, axis=1, keepdims=True)
    pick = jnp.sum(chosen * iota(chosen.shape, 1).astype(F32), axis=1, keepdims=True)
    lane = iota((kmax, BLOCK), 1)
    repeat = ((lax.rem(lane, LISTS) == iota((kmax, BLOCK), 0)) & (lane < 3 * LISTS)).astype(F32)
    listed = dot(dot(chosen, neighbors_ref[:, 0, :].astype(F32), 1), repeat, 0)
    lane = iota(listed.shape, 1)
    live = lax.rem(lane, LISTS).astype(F32) < count
    found = jnp.where(lane == PICK_LANE, pick, jnp.where(live, listed, float(cblocks)))
    table_ref[0 : 2 * TILE, :] = found.astype(I32)
    table_ref[2 * TILE : 3 * TILE, :] = jnp.zeros((TILE, BLOCK), I32)
    table_ref[2 * TILE : 2 * TILE + 1, 0:blocks] = place.astype(I32)
    to_scalar = pltpu.make_async_copy(table_ref, table, load_sem.at[2])
    to_scalar.start()

    def match_blocks(b, carry):
        listed = table_ref[pl.ds(slot_row(b, homes), 1), 0 : 4 * LISTS]
        lane = iota((cblocks, 4 * LISTS), 1)
        match = ((iota((cblocks, 4 * LISTS), 0) == listed) & (lane < 3 * LISTS)).astype(F32)
        absent = 1.0 - jnp.sum(jnp.where(lane < LISTS, match, 0.0), axis=1, keepdims=True)
        onehot[b] = jnp.where(lane == 3 * LISTS, absent, match).astype(BF16)
        return carry

    lax.fori_loop(0, slots, match_blocks, 0)

    loads[0].wait()

    def norm_row(i, carry):
        true_norm[pl.ds(i, 1), :] = square_norms(block_of(true, i)) * (UNIT / width)
        return carry

    lax.fori_loop(0, cblocks, norm_row, 0, unroll=8)
    loads[1].wait()
    to_scalar.wait()
    pred_norm[...] = jnp.zeros((TILE, BLOCK), F32)
    for b in range(homes):
        pred_norm[b : b + 1, :] = square_norms(block_of(pred, table[b, PICK_LANE])) * (UNIT / width)

    def products(b, carry):
        at = slot_row(b, homes)
        mine = jnp.transpose(block_of(pred, table[at, PICK_LANE]))
        for k in range(neighbors_ref.shape[0]):
            other = block_of(true, jnp.minimum(table[at, k], cblocks - 1))
            cost[b * kmax + k] = dot(mine, other, 0) * (2.0 * UNIT / width)
        return carry

    lax.fori_loop(0, slots, products, 0)


def sinkhorn_kernel(
    sizes, table, onehot, cost, pred_norm, true_norm, pred_out, true_out,
    potential, home_cols, spill_cols, pot_cols, tops, sums, spread,
    halves, half_in, merged, parts, share, swap_out, swap_in, last_out, last_in,
    half_send, half_recv, part_send, part_recv, share_send, share_recv, swap_send, swap_recv, last_send, last_recv,
):
    nz, ncol, homes, kmax, log_a, log_b = sizes
    row, col = lax.axis_index("row"), lax.axis_index("col")
    z, core = row // CORES, lax.rem(row, CORES)
    slots = 2 * homes
    cblocks = true_norm.shape[0]
    right, left = lax.rem(col + 1, ncol), lax.rem(col + (ncol - 1), ncol)
    mate = {"row": z * CORES + (1 - core)}
    piece = cblocks // (OWNERS * CORES)
    half = OWNERS * piece

    def far_first(i, n):
        return n // 2 + (1 - 2 * lax.rem(i, 2)) * ((i + 1) // 2)

    def along_z(d, c):
        return {"row": lax.rem(z + d, nz) * CORES + c}

    def ahead(i):
        return jnp.where(i == 0, 1, nz - i)

    def first_block(chip, c):
        return lax.rem(chip, OWNERS) * (CORES * piece) + c * piece

    barrier = pltpu.get_barrier_semaphore()

    def greet(device):
        pl.semaphore_signal(barrier, inc=1, device_id=device, device_id_type=MESH)

    def greet_z(i, carry):
        greet(along_z(i, core))
        return carry

    def greet_col(i, carry):
        greet({"col": lax.rem(col + i, ncol)})
        return carry

    lax.fori_loop(1, nz, greet_z, 0)
    lax.fori_loop(1, ncol, greet_col, 0)
    near = sorted({d % nz for d in (1, -1, 2, -2)})
    for d in near:
        greet(along_z(d, 1 - core))
    greet(mate)
    greeted = nz - 1 + ncol - 1 + len(near) + 1

    for step in range(ITERS):
        potential[step, cblocks : cblocks + TILE, :] = jnp.full((TILE, BLOCK), NEGATIVE, F32)
    home_cols[...] = jnp.zeros((BLOCK, BLOCK), F32)
    spill_cols[...] = jnp.zeros((BLOCK, BLOCK), F32)

    def fill(b, carry):
        tops[b] = jnp.zeros((LISTS, BLOCK), F32)
        sums[b] = jnp.ones((LISTS, BLOCK), F32)
        return carry

    lax.fori_loop(0, slots, fill, 0)
    potential[0, 0:cblocks, :] = -true_norm[...]

    def half_copy(step):
        return pltpu.make_async_remote_copy(
            src_ref=halves.at[step, 1 - core],
            dst_ref=half_in.at[step],
            send_sem=half_send.at[step],
            recv_sem=half_recv.at[step],
            device_id=mate,
            device_id_type=MESH,
        )

    def part_copy(step, i, sending):
        d = far_first(i, nz)
        return pltpu.make_async_remote_copy(
            src_ref=merged.at[step, pl.ds(lax.rem(lax.rem(z + d, nz), OWNERS) * piece, piece)],
            dst_ref=parts.at[step, z if sending else lax.rem(z + (nz - d), nz)],
            send_sem=part_send.at[step, d],
            recv_sem=part_recv.at[step, d],
            device_id=along_z(d, core),
            device_id_type=MESH,
        )

    def share_copy(stage, i, sending):
        d, c = ahead(i // CORES), lax.rem(i, CORES)
        chip, from_core = (z, core) if sending else (lax.rem(z + (nz - d), nz), c)
        return pltpu.make_async_remote_copy(
            src_ref=share.at[stage],
            dst_ref=potential.at[stage, pl.ds(first_block(chip, from_core), piece)],
            send_sem=share_send.at[stage, i],
            recv_sem=share_recv.at[stage, (i - c) + from_core],
            device_id=along_z(d, c),
            device_id_type=MESH,
        )

    def share_mate(stage, sending):
        return pltpu.make_async_remote_copy(
            src_ref=share.at[stage],
            dst_ref=potential.at[stage, pl.ds(first_block(z, core if sending else 1 - core), piece)],
            send_sem=share_send.at[stage, CORES * (OWNERS - 1)],
            recv_sem=share_recv.at[stage, CORES * (OWNERS - 1)],
            device_id=mate,
            device_id_type=MESH,
        )

    def swap_copy(step, spilled):
        return pltpu.make_async_remote_copy(
            src_ref=swap_out.at[step, pl.ds(TILE if spilled else 0, TILE)],
            dst_ref=swap_in.at[step, pl.ds(0 if spilled else TILE, TILE)],
            send_sem=swap_send.at[step, spilled],
            recv_sem=swap_recv.at[step, spilled],
            device_id={"col": left if spilled else right},
            device_id_type=MESH,
        )

    def last_copy(i, sending):
        d = far_first(i, ncol)
        return pltpu.make_async_remote_copy(
            src_ref=last_out,
            dst_ref=last_in.at[pl.ds(TILE * (col if sending else lax.rem(col + (ncol - d), ncol)), TILE)],
            send_sem=last_send.at[d],
            recv_sem=last_recv.at[d],
            device_id={"col": lax.rem(col + d, ncol)},
            device_id_type=MESH,
        )

    def each(count, action):
        def body(i, carry):
            action(i)
            return carry

        lax.fori_loop(0, count, body, 0)

    def iteration(step, carry):
        def over_true(cols):
            def body(b, carry):
                at = slot_row(b, homes)
                near = [potential[step, pl.ds(table[at, k], 1), :] for k in range(kmax)]
                for i in range(BLOCK // ROWS):
                    here = slice(i * ROWS, (i + 1) * ROWS)
                    top, total = top_and_total([cost[b * kmax + k, here, :] + near[k] for k in range(kmax)])
                    high = jnp.max(top, axis=1, keepdims=True)
                    total = jnp.sum(total * jnp.exp2(top - high), axis=1, keepdims=True)
                    cols[here, :] = jnp.where(iota((ROWS, BLOCK), 1) == lax.rem(at, TILE), high + jnp.log2(total), cols[here, :])
                return carry

            return body

        for spilled, cols in ((0, home_cols), (1, spill_cols)):
            lax.fori_loop(spilled * homes, (1 + spilled) * homes, over_true(cols), 0)
            swap_out[step, spilled * TILE : (1 + spilled) * TILE, :] = jnp.transpose(cols[...])[0:TILE, :]
            if not spilled:

                @pl.when(step == 0)
                def _():
                    pl.semaphore_wait(barrier, greeted)

            swap_copy(step, spilled).start()

        def over_pred(b, carry):
            at = lax.rem(slot_row(b, homes), TILE)
            mine = []
            for i in range(BLOCK // TILE):
                held = pot_cols[i * TILE : (i + 1) * TILE, :]
                picked = jnp.sum(jnp.where(iota((TILE, BLOCK), 1) == at, held, 0.0), axis=1, keepdims=True)
                mine.append(jnp.broadcast_to(picked, (TILE, BLOCK)))
            for k in range(kmax):
                top, total = top_and_total(
                    [cost[b * kmax + k, i * TILE : (i + 1) * TILE, :] + mine[i] for i in range(BLOCK // TILE)]
                )
                high = jnp.max(top, axis=0, keepdims=True)
                tops[b, k : k + 1, :] = high
                sums[b, k : k + 1, :] = jnp.sum(total * jnp.exp2(top - high), axis=0, keepdims=True)
            return carry

        for spilled in (1, 0):
            swap_copy(step, 1 - spilled).wait_recv()
            rows = slice(spilled * TILE, (1 + spilled) * TILE)
            pred_rows = log_a - join(swap_out[step, rows, :], swap_in[step, rows, :])
            if not spilled:

                @pl.when(step == ITERS - 1)
                def _():
                    final = (pred_rows + pred_norm[...]) * (1.0 / UNIT)
                    last_out[...] = final
                    last_in[pl.ds(pl.multiple_of(TILE * col, TILE), TILE), :] = final
                    each(ncol - 1, lambda i: last_copy(i, True).start())

            pot_cols[...] = jnp.transpose(jnp.concatenate([pred_rows, jnp.zeros((BLOCK - TILE, BLOCK), F32)], axis=0))
            lax.fori_loop(spilled * homes, (1 + spilled) * homes, over_pred, 0)

        for b in range(slots):
            value = tops[b] + jnp.log2(sums[b])
            first = value.astype(BF16)
            rest = value - first.astype(F32)
            second = rest.astype(BF16)
            third = (rest - second.astype(F32)).astype(BF16)
            none = jnp.where(iota((LISTS, BLOCK), 0) == 0, NEGATIVE, 0.0).astype(BF16)
            spread[b] = dot(onehot[b], jnp.concatenate([first, second, third, none], axis=0), 0)

        def gather(which):
            for g in range(OWNERS):
                top, total = top_and_total(
                    [spread[b, pl.ds(pl.multiple_of(first_block(g, which), piece), piece), :] for b in range(slots)]
                )
                halves[step, which, g * piece : (g + 1) * piece, :] = top + jnp.log2(total)

        gather(1 - core)
        half_copy(step).start()
        gather(core)
        half_copy(step).wait_recv()
        merged[step] = join(halves[step, core], half_in[step])
        each(nz - 1, lambda i: part_copy(step, i, True).start())
        parts[step, z] = merged[step, pl.ds(pl.multiple_of(lax.rem(z, OWNERS) * piece, piece), piece), :]
        each(nz - 1, lambda i: part_copy(step, nz - 2 - i, False).wait_recv())
        top, total = top_and_total([parts[step, i] for i in range(nz)])
        fresh = log_b - (top + jnp.log2(total))
        own = pl.ds(pl.multiple_of(first_block(z, core), piece), piece)
        fresh = jnp.where(step == ITERS - 1, (fresh + true_norm[own, :]) * (1.0 / UNIT), fresh)
        share[step + 1] = fresh
        potential[step + 1, own, :] = fresh
        each(CORES * (OWNERS - 1), lambda i: share_copy(step + 1, CORES * (OWNERS - 1) - 1 - i, True).start())
        share_mate(step + 1, True).start()

        @pl.when(step == ITERS - 1)
        def _():
            each(ncol - 1, lambda i: last_copy(i, False).wait_recv())

            def place(i, carry):
                pred_out[pl.ds(i, 1), :] = last_in[pl.ds(table[2 * TILE, i], 1), :]
                return carry

            lax.fori_loop(0, pred_out.shape[0], place, 0, unroll=8)
            each(ncol - 1, lambda i: last_copy(i, True).wait_send())

        half_copy(step).wait_send()
        for spilled in (0, 1):
            swap_copy(step, spilled).wait_send()
        each(nz - 1, lambda i: part_copy(step, i, True).wait_send())
        share_mate(step + 1, False).wait_recv()
        each(CORES * (OWNERS - 1), lambda i: share_copy(step + 1, i, False).wait_recv())
        return carry

    lax.fori_loop(0, ITERS, iteration, 0)
    true_out[...] = potential[ITERS, 0:cblocks, :]

    def sent(stage, carry):
        each(CORES * (OWNERS - 1), lambda i: share_copy(stage, i, True).wait_send())
        share_mate(stage, True).wait_send()
        return carry

    lax.fori_loop(1, ITERS + 1, sent, 0)


def on_device(pred_feat, true_feat, neighbors, counts):
    width = pred_feat.shape[1]
    rblocks, cblocks = pred_feat.shape[0] // BLOCK, true_feat.shape[0] // BLOCK
    nrow, ncol = lax.axis_size("row"), lax.axis_size("col")
    nz, homes, kmax = nrow // CORES, rblocks // ncol, neighbors.shape[2]
    slots, half = 2 * homes, cblocks // CORES
    piece = half // OWNERS
    log_a = -math.log2(pred_feat.shape[0] * nrow)
    log_b = -math.log2(true_feat.shape[0] * ncol)
    vmem = pl.BlockSpec(memory_space=pltpu.VMEM)
    anywhere = pl.BlockSpec(memory_space=pl.ANY)
    dma = pltpu.SemaphoreType.DMA
    ready = pl.pallas_call(
        functools.partial(prepare_kernel, ncol, homes),
        out_shape=(
            jax.ShapeDtypeStruct((3 * TILE, BLOCK), I32),
            jax.ShapeDtypeStruct((slots, cblocks, 4 * LISTS), BF16),
            jax.ShapeDtypeStruct((slots * kmax, BLOCK, BLOCK), F32),
            jax.ShapeDtypeStruct((TILE, BLOCK), F32),
            jax.ShapeDtypeStruct((cblocks, BLOCK), F32),
        ),
        in_specs=[vmem, vmem, anywhere, anywhere],
        out_specs=(vmem,) * 5,
        scratch_shapes=[
            pltpu.VMEM((width, rblocks * BLOCK), BF16),
            pltpu.VMEM((width, cblocks * BLOCK), BF16),
            pltpu.SMEM((3 * TILE, BLOCK), I32),
            dma((3,)),
        ],
        compiler_params=pltpu.CompilerParams(vmem_limit_bytes=24 * 2**20),
        name="prepare",
    )(counts.T, jnp.transpose(neighbors, (2, 1, 0)), pred_feat.T, true_feat.T)
    pred_pot, true_pot = pl.pallas_call(
        functools.partial(sinkhorn_kernel, (nz, ncol, homes, kmax, log_a, log_b)),
        out_shape=(
            jax.ShapeDtypeStruct((rblocks, BLOCK), F32),
            jax.ShapeDtypeStruct((cblocks, BLOCK), F32),
        ),
        in_specs=[
            pl.BlockSpec(memory_space=pltpu.SMEM),
            vmem,
            vmem,
            vmem,
            vmem,
        ],
        out_specs=(vmem, vmem),
        scratch_shapes=[
            pltpu.VMEM((ITERS + 1, cblocks + TILE, BLOCK), F32),
            pltpu.VMEM((BLOCK, BLOCK), F32),
            pltpu.VMEM((BLOCK, BLOCK), F32),
            pltpu.VMEM((BLOCK, BLOCK), F32),
            pltpu.VMEM((slots, LISTS, BLOCK), F32),
            pltpu.VMEM((slots, LISTS, BLOCK), F32),
            pltpu.VMEM((slots, cblocks, BLOCK), F32),
            pltpu.VMEM((ITERS, CORES, half, BLOCK), F32),
            pltpu.VMEM((ITERS, half, BLOCK), F32),
            pltpu.VMEM((ITERS, half, BLOCK), F32),
            pltpu.VMEM((ITERS, nz, piece, BLOCK), F32),
            pltpu.VMEM((ITERS + 1, piece, BLOCK), F32),
            pltpu.VMEM((ITERS, 2 * TILE, BLOCK), F32),
            pltpu.VMEM((ITERS, 2 * TILE, BLOCK), F32),
            pltpu.VMEM((TILE, BLOCK), F32),
            pltpu.VMEM((TILE * ncol, BLOCK), F32),
            dma((ITERS,)),
            dma((ITERS,)),
            dma((ITERS, nz)),
            dma((ITERS, nz)),
            dma((ITERS + 1, CORES * (OWNERS - 1) + 1)),
            dma((ITERS + 1, CORES * (OWNERS - 1) + 1)),
            dma((ITERS, 2)),
            dma((ITERS, 2)),
            dma((ncol,)),
            dma((ncol,)),
        ],
        compiler_params=pltpu.CompilerParams(
            collective_id=0, has_side_effects=True, vmem_limit_bytes=24 * 2**20
        ),
        name="sinkhorn",
    )(*ready)
    return (pred_pot.reshape(-1), true_pot.reshape(-1))


def solution(mesh):
    in_specs = (P("row", None), P("col", None), P("row", "col", None), P("row", None))
    out_specs = (P("row"), P("col"))
    return jax.shard_map(
        on_device, mesh=mesh, in_specs=in_specs, out_specs=out_specs, check_vma=False
    )
```

```python
import functools
import math

import jax
import jax.numpy as jnp
from jax import lax
from jax.experimental import pallas as pl
from jax.experimental.pallas import tpu as pltpu
from jax.sharding import PartitionSpec as P

BLOCK = 128
ITERS = 3
EPSILON = 0.02
NEGATIVE = -1e30
TILE = 8
CORES = 2
ROWS = 16
OWNERS = 4
LISTS = 16
PICK_LANE = 63
UNIT = 1.0 / (EPSILON * math.log(2.0))
MESH = pl.DeviceIdType.MESH
F32, BF16, I32 = jnp.float32, jnp.bfloat16, jnp.int32


def dot(a, b, b_axis):
    return lax.dot_general(a, b, (((1,), (b_axis,)), ((), ())), preferred_element_type=F32)


def iota(shape, axis):
    return lax.broadcasted_iota(I32, shape, axis)


def join(a, b):
    high, low = jnp.maximum(a, b), jnp.minimum(a, b)
    return high + jnp.log2(1.0 + jnp.exp2(low - high))


def tree(op, items):
    items = list(items)
    while len(items) > 1:
        items = [op(*items[i : i + 2]) if i + 1 < len(items) else items[i] for i in range(0, len(items), 2)]
    return items[0]


def top_and_total(items):
    top = tree(jnp.maximum, items)
    return top, tree(jnp.add, [jnp.exp2(item - top) for item in items])


def square_norms(block):
    wide = block.astype(F32)
    return jnp.sum(wide * wide, axis=0, keepdims=True)


def block_of(features, index):
    return features[:, pl.ds(pl.multiple_of(BLOCK * index, BLOCK), BLOCK)]


def slot_row(b, homes):
    return jnp.where(b < homes, b, b + (TILE - homes))


def prepare_kernel(
    ncol, homes, counts_ref, neighbors_ref, pred, true, table_ref, onehot, cost, pred_norm, true_norm,
    table, copied,
):
    here = lax.axis_index("col")
    width, cblocks = true.shape[0], true_norm.shape[0]
    slots = 2 * homes
    counts = counts_ref[...].astype(F32)
    blocks, kmax = counts.shape[1], neighbors_ref.shape[0]
    to, frm = iota((ncol, ncol), 0), iota((ncol, ncol), 1)
    before = (frm == lax.rem(to + (ncol - 1), ncol)).astype(F32)
    home = ((counts > 0.5) & (dot(before, counts, 0) < 0.5)).astype(F32)
    upto = (iota((blocks, blocks), 0) <= iota((blocks, blocks), 1)).astype(F32)
    rank = dot(home, upto, 0) - 1.0
    shard = iota(home.shape, 0).astype(F32)
    place = jnp.sum(home * (TILE * shard + rank), axis=0, keepdims=True)
    slot = iota((2 * TILE, blocks), 0)
    owner = jnp.where(slot < TILE, here, lax.rem(here + (ncol - 1), ncol))
    wanted = (TILE * owner + lax.rem(slot, TILE)).astype(F32)
    chosen = (place == wanted).astype(F32)
    count = jnp.sum(jnp.where(iota(counts.shape, 0) == here, counts, 0.0), axis=0, keepdims=True)
    count = jnp.sum(chosen * count, axis=1, keepdims=True)
    pick = jnp.sum(chosen * iota(chosen.shape, 1).astype(F32), axis=1, keepdims=True)
    lane = iota((kmax, BLOCK), 1)
    repeat = ((lax.rem(lane, LISTS) == iota((kmax, BLOCK), 0)) & (lane < 3 * LISTS)).astype(F32)
    listed = dot(dot(chosen, neighbors_ref[:, 0, :].astype(F32), 1), repeat, 0)
    lane = iota(listed.shape, 1)
    live = lax.rem(lane, LISTS).astype(F32) < count
    found = jnp.where(lane == PICK_LANE, pick, jnp.where(live, listed, float(cblocks)))
    table_ref[0 : 2 * TILE, :] = found.astype(I32)
    table_ref[2 * TILE : 3 * TILE, :] = jnp.zeros((TILE, BLOCK), I32)
    table_ref[2 * TILE : 2 * TILE + 1, 0:blocks] = place.astype(I32)
    to_scalar = pltpu.make_async_copy(table_ref, table, copied)
    to_scalar.start()

    def match_blocks(b, carry):
        listed = table_ref[pl.ds(slot_row(b, homes), 1), 0 : 4 * LISTS]
        lane = iota((cblocks, 4 * LISTS), 1)
        match = ((iota((cblocks, 4 * LISTS), 0) == listed) & (lane < 3 * LISTS)).astype(F32)
        absent = 1.0 - jnp.sum(jnp.where(lane < LISTS, match, 0.0), axis=1, keepdims=True)
        onehot[b] = jnp.where(lane == 3 * LISTS, absent, match).astype(BF16)
        return carry

    lax.fori_loop(0, slots, match_blocks, 0)

    def norm_row(i, carry):
        true_norm[pl.ds(i, 1), :] = square_norms(block_of(true, i)) * (UNIT / width)
        return carry

    lax.fori_loop(0, cblocks, norm_row, 0, unroll=8)
    to_scalar.wait()
    pred_norm[...] = jnp.zeros((TILE, BLOCK), F32)
    for b in range(homes):
        pred_norm[b : b + 1, :] = square_norms(block_of(pred, table[b, PICK_LANE])) * (UNIT / width)

    def products(b, carry):
        at = slot_row(b, homes)
        mine = jnp.transpose(block_of(pred, table[at, PICK_LANE]))
        for k in range(neighbors_ref.shape[0]):
            other = block_of(true, jnp.minimum(table[at, k], cblocks - 1))
            cost[b * kmax + k] = dot(mine, other, 0) * (2.0 * UNIT / width)
        return carry

    lax.fori_loop(0, slots, products, 0)


def sinkhorn_kernel(
    sizes, table, onehot, cost, pred_norm, true_norm, pred_out, true_out,
    potential, held, tops, sums, spread,
    halves, half_in, merged, parts, share, swap_out, swap_in, last_out, last_in,
    half_send, half_recv, part_send, part_recv, share_send, share_recv, swap_send, swap_recv, last_send, last_recv,
):
    nz, ncol, homes, kmax, log_a, log_b = sizes
    row, col = lax.axis_index("row"), lax.axis_index("col")
    z, core = row // CORES, lax.rem(row, CORES)
    slots = 2 * homes
    cblocks = true_norm.shape[0]
    right, left = lax.rem(col + 1, ncol), lax.rem(col + (ncol - 1), ncol)
    mate = {"row": z * CORES + (1 - core)}
    piece = cblocks // (OWNERS * CORES)
    half = OWNERS * piece

    def far_first(i, n):
        return n // 2 + (1 - 2 * lax.rem(i, 2)) * ((i + 1) // 2)

    def along_z(d, c):
        return {"row": lax.rem(z + d, nz) * CORES + c}

    def ahead(i):
        return jnp.where(i == 0, 1, nz - i)

    def first_block(chip, c):
        return lax.rem(chip, OWNERS) * (CORES * piece) + c * piece

    barrier = pltpu.get_barrier_semaphore()

    def greet(device):
        pl.semaphore_signal(barrier, inc=1, device_id=device, device_id_type=MESH)

    def greet_z(i, carry):
        greet(along_z(i, core))
        return carry

    def greet_col(i, carry):
        greet({"col": lax.rem(col + i, ncol)})
        return carry

    lax.fori_loop(1, nz, greet_z, 0)
    lax.fori_loop(1, ncol, greet_col, 0)
    near = sorted({d % nz for d in (1, -1, 2, -2)})
    for d in near:
        greet(along_z(d, 1 - core))
    greet(mate)
    greeted = nz - 1 + ncol - 1 + len(near) + 1

    for step in range(ITERS):
        potential[step, cblocks : cblocks + TILE, :] = jnp.full((TILE, BLOCK), NEGATIVE, F32)
    swap_out[...] = jnp.zeros(swap_out.shape, F32)
    tops[...] = jnp.zeros(tops.shape, F32)
    sums[...] = jnp.ones(sums.shape, F32)
    potential[0, 0:cblocks, :] = -true_norm[...]

    def half_copy(step):
        return pltpu.make_async_remote_copy(
            src_ref=halves.at[step, 1 - core],
            dst_ref=half_in.at[step],
            send_sem=half_send.at[step],
            recv_sem=half_recv.at[step],
            device_id=mate,
            device_id_type=MESH,
        )

    def part_copy(step, i, sending):
        d = far_first(i, nz)
        return pltpu.make_async_remote_copy(
            src_ref=merged.at[step, pl.ds(lax.rem(lax.rem(z + d, nz), OWNERS) * piece, piece)],
            dst_ref=parts.at[step, z if sending else lax.rem(z + (nz - d), nz)],
            send_sem=part_send.at[step, d],
            recv_sem=part_recv.at[step, d],
            device_id=along_z(d, core),
            device_id_type=MESH,
        )

    def share_copy(stage, i, sending):
        d, c = ahead(i // CORES), lax.rem(i, CORES)
        chip, from_core = (z, core) if sending else (lax.rem(z + (nz - d), nz), c)
        return pltpu.make_async_remote_copy(
            src_ref=share.at[stage],
            dst_ref=potential.at[stage, pl.ds(first_block(chip, from_core), piece)],
            send_sem=share_send.at[stage, i],
            recv_sem=share_recv.at[stage, (i - c) + from_core],
            device_id=along_z(d, c),
            device_id_type=MESH,
        )

    def share_mate(stage, sending):
        return pltpu.make_async_remote_copy(
            src_ref=share.at[stage],
            dst_ref=potential.at[stage, pl.ds(first_block(z, core if sending else 1 - core), piece)],
            send_sem=share_send.at[stage, CORES * (OWNERS - 1)],
            recv_sem=share_recv.at[stage, CORES * (OWNERS - 1)],
            device_id=mate,
            device_id_type=MESH,
        )

    def swap_copy(step, spilled):
        return pltpu.make_async_remote_copy(
            src_ref=swap_out.at[step, pl.ds(TILE if spilled else 0, TILE)],
            dst_ref=swap_in.at[step, pl.ds(0 if spilled else TILE, TILE)],
            send_sem=swap_send.at[step, spilled],
            recv_sem=swap_recv.at[step, spilled],
            device_id={"col": left if spilled else right},
            device_id_type=MESH,
        )

    def last_copy(i, sending):
        d = far_first(i, ncol)
        return pltpu.make_async_remote_copy(
            src_ref=last_out,
            dst_ref=last_in.at[pl.ds(TILE * (col if sending else lax.rem(col + (ncol - d), ncol)), TILE)],
            send_sem=last_send.at[d],
            recv_sem=last_recv.at[d],
            device_id={"col": lax.rem(col + d, ncol)},
            device_id_type=MESH,
        )

    def each(count, action):
        def body(i, carry):
            action(i)
            return carry

        lax.fori_loop(0, count, body, 0)

    def iteration(step, carry):
        for spilled in (0, 1):
            for b in range(spilled * homes, (1 + spilled) * homes):
                at = b if b < homes else b + (TILE - homes)
                near = [potential[step, pl.ds(table[at, k], 1), :] for k in range(kmax)]
                found = [
                    top_and_total([cost[b * kmax + k, i : i + ROWS, :] + near[k] for k in range(kmax)])
                    for i in range(0, BLOCK, ROWS)
                ]
                top, total = (jnp.transpose(jnp.concatenate(part, axis=0)) for part in zip(*found))
                high = jnp.max(top, axis=0, keepdims=True)
                total = jnp.sum(total * jnp.exp2(top - high), axis=0, keepdims=True)
                swap_out[step, at : at + 1, :] = high + jnp.log2(total)
            if not spilled:

                @pl.when(step == 0)
                def _():
                    pl.semaphore_wait(barrier, greeted)

            swap_copy(step, spilled).start()

        def over_pred(b, carry):
            for k in range(kmax):
                top, total = top_and_total(
                    [
                        cost[b * kmax + k, i : i + TILE, :] + held[lax.rem(b, homes), i : i + TILE, :]
                        for i in range(0, BLOCK, TILE)
                    ]
                )
                high = jnp.max(top, axis=0, keepdims=True)
                tops[b, k : k + 1, :] = high
                sums[b, k : k + 1, :] = jnp.sum(total * jnp.exp2(top - high), axis=0, keepdims=True)
            return carry

        for spilled in (1, 0):
            swap_copy(step, 1 - spilled).wait_recv()
            rows = slice(spilled * TILE, (1 + spilled) * TILE)
            pred_rows = log_a - join(swap_out[step, rows, :], swap_in[step, rows, :])
            if not spilled:

                @pl.when(step == ITERS - 1)
                def _():
                    final = (pred_rows + pred_norm[...]) * (1.0 / UNIT)
                    last_out[...] = final
                    last_in[pl.ds(pl.multiple_of(TILE * col, TILE), TILE), :] = final
                    each(ncol - 1, lambda i: last_copy(i, True).start())

            across = jnp.transpose(jnp.concatenate([pred_rows, jnp.zeros((BLOCK - TILE, BLOCK), F32)], axis=0))
            for b in range(homes):
                held[b] = jnp.broadcast_to(across[:, b : b + 1], (BLOCK, BLOCK))
            lax.fori_loop(spilled * homes, (1 + spilled) * homes, over_pred, 0)

        for b in range(slots):
            value = tops[b] + jnp.log2(sums[b])
            first = value.astype(BF16)
            rest = value - first.astype(F32)
            second = rest.astype(BF16)
            third = (rest - second.astype(F32)).astype(BF16)
            none = jnp.where(iota((LISTS, BLOCK), 0) == 0, NEGATIVE, 0.0).astype(BF16)
            spread[b] = dot(onehot[b], jnp.concatenate([first, second, third, none], axis=0), 0)

        def gather(which):
            for g in range(OWNERS):
                top, total = top_and_total(
                    [spread[b, pl.ds(pl.multiple_of(first_block(g, which), piece), piece), :] for b in range(slots)]
                )
                halves[step, which, g * piece : (g + 1) * piece, :] = top + jnp.log2(total)

        gather(1 - core)
        half_copy(step).start()
        gather(core)
        half_copy(step).wait_recv()
        merged[step] = join(halves[step, core], half_in[step])
        each(nz - 1, lambda i: part_copy(step, i, True).start())
        parts[step, z] = merged[step, pl.ds(pl.multiple_of(lax.rem(z, OWNERS) * piece, piece), piece), :]
        each(nz - 1, lambda i: part_copy(step, nz - 2 - i, False).wait_recv())
        top, total = top_and_total([parts[step, i] for i in range(nz)])
        fresh = log_b - (top + jnp.log2(total))
        own = pl.ds(pl.multiple_of(first_block(z, core), piece), piece)
        fresh = jnp.where(step == ITERS - 1, (fresh + true_norm[own, :]) * (1.0 / UNIT), fresh)
        share[step + 1] = fresh
        potential[step + 1, own, :] = fresh
        each(CORES * (OWNERS - 1), lambda i: share_copy(step + 1, CORES * (OWNERS - 1) - 1 - i, True).start())
        share_mate(step + 1, True).start()

        @pl.when(step == ITERS - 1)
        def _():
            each(ncol - 1, lambda i: last_copy(i, False).wait_recv())

            def place(i, carry):
                pred_out[pl.ds(i, 1), :] = last_in[pl.ds(table[2 * TILE, i], 1), :]
                return carry

            lax.fori_loop(0, pred_out.shape[0], place, 0, unroll=8)
            each(ncol - 1, lambda i: last_copy(i, True).wait_send())

        half_copy(step).wait_send()
        for spilled in (0, 1):
            swap_copy(step, spilled).wait_send()
        each(nz - 1, lambda i: part_copy(step, i, True).wait_send())
        share_mate(step + 1, False).wait_recv()
        each(CORES * (OWNERS - 1), lambda i: share_copy(step + 1, i, False).wait_recv())
        return carry

    lax.fori_loop(0, ITERS, iteration, 0)
    true_out[...] = potential[ITERS, 0:cblocks, :]

    def sent(stage, carry):
        each(CORES * (OWNERS - 1), lambda i: share_copy(stage, i, True).wait_send())
        share_mate(stage, True).wait_send()
        return carry

    lax.fori_loop(1, ITERS + 1, sent, 0)


def on_device(pred_feat, true_feat, neighbors, counts):
    width = pred_feat.shape[1]
    rblocks, cblocks = pred_feat.shape[0] // BLOCK, true_feat.shape[0] // BLOCK
    nrow, ncol = lax.axis_size("row"), lax.axis_size("col")
    nz, homes, kmax = nrow // CORES, rblocks // ncol, neighbors.shape[2]
    slots, half = 2 * homes, cblocks // CORES
    piece = half // OWNERS
    log_a = -math.log2(pred_feat.shape[0] * nrow)
    log_b = -math.log2(true_feat.shape[0] * ncol)
    vmem = pl.BlockSpec(memory_space=pltpu.VMEM)
    dma = pltpu.SemaphoreType.DMA
    ready = pl.pallas_call(
        functools.partial(prepare_kernel, ncol, homes),
        out_shape=(
            jax.ShapeDtypeStruct((3 * TILE, BLOCK), I32),
            jax.ShapeDtypeStruct((slots, cblocks, 4 * LISTS), BF16),
            jax.ShapeDtypeStruct((slots * kmax, BLOCK, BLOCK), F32),
            jax.ShapeDtypeStruct((TILE, BLOCK), F32),
            jax.ShapeDtypeStruct((cblocks, BLOCK), F32),
        ),
        in_specs=[vmem] * 4,
        out_specs=(vmem,) * 5,
        scratch_shapes=[
            pltpu.SMEM((3 * TILE, BLOCK), I32),
            dma(()),
        ],
        compiler_params=pltpu.CompilerParams(vmem_limit_bytes=24 * 2**20),
        name="prepare",
    )(counts.T, jnp.transpose(neighbors, (2, 1, 0)), pred_feat.T, true_feat.T)
    pred_pot, true_pot = pl.pallas_call(
        functools.partial(sinkhorn_kernel, (nz, ncol, homes, kmax, log_a, log_b)),
        out_shape=(
            jax.ShapeDtypeStruct((rblocks, BLOCK), F32),
            jax.ShapeDtypeStruct((cblocks, BLOCK), F32),
        ),
        in_specs=[
            pl.BlockSpec(memory_space=pltpu.SMEM),
            vmem,
            vmem,
            vmem,
            vmem,
        ],
        out_specs=(vmem, vmem),
        scratch_shapes=[
            pltpu.VMEM((ITERS + 1, cblocks + TILE, BLOCK), F32),
            pltpu.VMEM((homes, BLOCK, BLOCK), F32),
            pltpu.VMEM((slots, LISTS, BLOCK), F32),
            pltpu.VMEM((slots, LISTS, BLOCK), F32),
            pltpu.VMEM((slots, cblocks, BLOCK), F32),
            pltpu.VMEM((ITERS, CORES, half, BLOCK), F32),
            pltpu.VMEM((ITERS, half, BLOCK), F32),
            pltpu.VMEM((ITERS, half, BLOCK), F32),
            pltpu.VMEM((ITERS, nz, piece, BLOCK), F32),
            pltpu.VMEM((ITERS + 1, piece, BLOCK), F32),
            pltpu.VMEM((ITERS, 2 * TILE, BLOCK), F32),
            pltpu.VMEM((ITERS, 2 * TILE, BLOCK), F32),
            pltpu.VMEM((TILE, BLOCK), F32),
            pltpu.VMEM((TILE * ncol, BLOCK), F32),
            dma((ITERS,)),
            dma((ITERS,)),
            dma((ITERS, nz)),
            dma((ITERS, nz)),
            dma((ITERS + 1, CORES * (OWNERS - 1) + 1)),
            dma((ITERS + 1, CORES * (OWNERS - 1) + 1)),
            dma((ITERS, 2)),
            dma((ITERS, 2)),
            dma((ncol,)),
            dma((ncol,)),
        ],
        compiler_params=pltpu.CompilerParams(
            collective_id=0, has_side_effects=True, vmem_limit_bytes=24 * 2**20
        ),
        name="sinkhorn",
    )(*ready)
    return (pred_pot.reshape(-1), true_pot.reshape(-1))


def solution(mesh):
    in_specs = (P("row", None), P("col", None), P("row", "col", None), P("row", None))
    out_specs = (P("row"), P("col"))
    return jax.shard_map(
        on_device, mesh=mesh, in_specs=in_specs, out_specs=out_specs, check_vma=False
    )
```

```python
import functools
import math

import jax
import jax.numpy as jnp
from jax import lax
from jax.experimental import pallas as pl
from jax.experimental.pallas import tpu as pltpu
from jax.sharding import PartitionSpec as P

BLOCK = 128
ITERS = 3
EPSILON = 0.02
NEGATIVE = -1e30
TILE = 8
CORES = 2
ROWS = 16
OWNERS = 4
LISTS = 16
PICK_LANE = 63
UNIT = 1.0 / (EPSILON * math.log(2.0))
MESH = pl.DeviceIdType.MESH
F32, BF16, I32 = jnp.float32, jnp.bfloat16, jnp.int32


def dot(a, b, b_axis):
    return lax.dot_general(a, b, (((1,), (b_axis,)), ((), ())), preferred_element_type=F32)


def iota(shape, axis):
    return lax.broadcasted_iota(I32, shape, axis)


def join(a, b):
    high, low = jnp.maximum(a, b), jnp.minimum(a, b)
    return high + jnp.log2(1.0 + jnp.exp2(low - high))


def tree(op, items):
    items = list(items)
    while len(items) > 1:
        items = [op(*items[i : i + 2]) if i + 1 < len(items) else items[i] for i in range(0, len(items), 2)]
    return items[0]


def top_and_total(items):
    top = tree(jnp.maximum, items)
    return top, tree(jnp.add, [jnp.exp2(item - top) for item in items])


def square_norms(block):
    wide = block.astype(F32)
    return jnp.sum(wide * wide, axis=0, keepdims=True)


def slot_row(b, homes):
    return b if b < homes else b + (TILE - homes)


def prepare_kernel(ncol, homes, counts_ref, neighbors_ref, table_ref, onehot):
    here = lax.axis_index("col")
    cblocks = onehot.shape[1]
    counts = counts_ref[...].astype(F32)
    blocks, kmax = counts.shape[1], neighbors_ref.shape[0]
    to, frm = iota((ncol, ncol), 0), iota((ncol, ncol), 1)
    before = (frm == lax.rem(to + (ncol - 1), ncol)).astype(F32)
    home = ((counts > 0.5) & (dot(before, counts, 0) < 0.5)).astype(F32)
    upto = (iota((blocks, blocks), 0) <= iota((blocks, blocks), 1)).astype(F32)
    rank = dot(home, upto, 0) - 1.0
    shard = iota(home.shape, 0).astype(F32)
    place = jnp.sum(home * (TILE * shard + rank), axis=0, keepdims=True)
    slot = iota((2 * TILE, blocks), 0)
    owner = jnp.where(slot < TILE, here, lax.rem(here + (ncol - 1), ncol))
    wanted = (TILE * owner + lax.rem(slot, TILE)).astype(F32)
    chosen = (place == wanted).astype(F32)
    count = jnp.sum(jnp.where(iota(counts.shape, 0) == here, counts, 0.0), axis=0, keepdims=True)
    count = jnp.sum(chosen * count, axis=1, keepdims=True)
    pick = jnp.sum(chosen * iota(chosen.shape, 1).astype(F32), axis=1, keepdims=True)
    lane = iota((kmax, BLOCK), 1)
    repeat = ((lax.rem(lane, LISTS) == iota((kmax, BLOCK), 0)) & (lane < 3 * LISTS)).astype(F32)
    listed = dot(dot(chosen, neighbors_ref[:, 0, :].astype(F32), 1), repeat, 0)
    lane = iota(listed.shape, 1)
    live = lax.rem(lane, LISTS).astype(F32) < count
    found = jnp.where(lane == PICK_LANE, pick, jnp.where(live, listed, float(cblocks)))
    table_ref[0 : 2 * TILE, :] = found.astype(I32)
    table_ref[2 * TILE : 3 * TILE, :] = jnp.zeros((TILE, BLOCK), I32)
    table_ref[2 * TILE : 2 * TILE + 1, 0:blocks] = place.astype(I32)
    first_named = jnp.where(lane == PICK_LANE, pick, jnp.where(live, listed, 0.0))
    table_ref[3 * TILE : 5 * TILE, :] = first_named.astype(I32)

    for b in range(2 * homes):
        at = slot_row(b, homes)
        listed = table_ref[at : at + 1, 0 : 4 * LISTS]
        lane = iota((cblocks, 4 * LISTS), 1)
        match = ((iota((cblocks, 4 * LISTS), 0) == listed) & (lane < 3 * LISTS)).astype(F32)
        absent = 1.0 - jnp.sum(jnp.where(lane < LISTS, match, 0.0), axis=1, keepdims=True)
        onehot[b] = jnp.where(lane == 3 * LISTS, absent, match).astype(BF16)


def sinkhorn_kernel(
    sizes, table, onehot_hbm, pred_hbm, true_hbm, pred_out, true_out,
    pred, true, pred_blocks, true_blocks, onehot, cost, pred_norm, true_norm,
    potential, held, tops, sums, spread,
    halves, half_in, merged, parts, share, swap_out, swap_in, last_out, last_in,
    load_sem, half_send, half_recv, part_send, part_recv, share_send, share_recv, swap_send, swap_recv, last_send, last_recv,
):
    nz, ncol, homes, kmax, log_a, log_b = sizes
    row, col = lax.axis_index("row"), lax.axis_index("col")
    z, core = row // CORES, lax.rem(row, CORES)
    slots = 2 * homes
    cblocks, width = true_norm.shape[0], true.shape[0]
    right, left = lax.rem(col + 1, ncol), lax.rem(col + (ncol - 1), ncol)
    mate = {"row": z * CORES + (1 - core)}
    piece = cblocks // (OWNERS * CORES)
    half = OWNERS * piece

    def far_first(i, n):
        return n // 2 + (1 - 2 * lax.rem(i, 2)) * ((i + 1) // 2)

    def along_z(d, c):
        return {"row": lax.rem(z + d, nz) * CORES + c}

    def ahead(i):
        return jnp.where(i == 0, 1, nz - i)

    def first_block(chip, c):
        return lax.rem(chip, OWNERS) * (CORES * piece) + c * piece

    loads = [
        pltpu.make_async_copy(true_hbm, true, load_sem.at[0]),
        pltpu.make_async_copy(pred_hbm, pred, load_sem.at[1]),
        pltpu.make_async_copy(onehot_hbm, onehot, load_sem.at[2]),
    ]
    for load in loads:
        load.start()

    barrier = pltpu.get_barrier_semaphore()

    def greet(device):
        pl.semaphore_signal(barrier, inc=1, device_id=device, device_id_type=MESH)

    def greet_z(i, carry):
        greet(along_z(i, core))
        return carry

    def greet_col(i, carry):
        greet({"col": lax.rem(col + i, ncol)})
        return carry

    lax.fori_loop(1, nz, greet_z, 0)
    lax.fori_loop(1, ncol, greet_col, 0)
    near = sorted({d % nz for d in (1, -1, 2, -2)})
    for d in near:
        greet(along_z(d, 1 - core))
    greet(mate)
    greeted = nz - 1 + ncol - 1 + len(near) + 1

    for step in range(ITERS):
        potential[step, cblocks : cblocks + TILE, :] = jnp.full((TILE, BLOCK), NEGATIVE, F32)
    swap_out[...] = jnp.zeros(swap_out.shape, F32)
    tops[...] = jnp.zeros(tops.shape, F32)
    sums[...] = jnp.ones(sums.shape, F32)
    pred_norm[...] = jnp.zeros(pred_norm.shape, F32)
    loads[0].wait()

    def take_true(i, carry):
        block = true[:, pl.ds(pl.multiple_of(BLOCK * i, BLOCK), BLOCK)]
        true_blocks[i] = block
        true_norm[pl.ds(i, 1), :] = square_norms(block) * (UNIT / width)
        return carry

    lax.fori_loop(0, cblocks, take_true, 0, unroll=16)
    potential[0, 0:cblocks, :] = -true_norm[...]
    loads[1].wait()

    def take_pred(i, carry):
        pred_blocks[i] = pred[:, pl.ds(pl.multiple_of(BLOCK * i, BLOCK), BLOCK)]
        return carry

    lax.fori_loop(0, pred_out.shape[0], take_pred, 0, unroll=16)
    loads[2].wait()
    for b in range(homes):
        pred_norm[b : b + 1, :] = square_norms(pred_blocks[table[b, PICK_LANE]]) * (UNIT / width)

    def products(b, carry):
        at = 3 * TILE + jnp.where(b < homes, b, b + (TILE - homes))
        mine = jnp.transpose(pred_blocks[table[at, PICK_LANE]])
        for k in range(kmax):
            cost[b * kmax + k] = dot(mine, true_blocks[table[at, k]], 0) * (2.0 * UNIT / width)
        return carry

    lax.fori_loop(0, slots, products, 0)

    def half_copy(step):
        return pltpu.make_async_remote_copy(
            src_ref=halves.at[step, 1 - core],
            dst_ref=half_in.at[step],
            send_sem=half_send.at[step],
            recv_sem=half_recv.at[step],
            device_id=mate,
            device_id_type=MESH,
        )

    def part_copy(step, i, sending):
        d = far_first(i, nz)
        return pltpu.make_async_remote_copy(
            src_ref=merged.at[step, pl.ds(lax.rem(lax.rem(z + d, nz), OWNERS) * piece, piece)],
            dst_ref=parts.at[step, z if sending else lax.rem(z + (nz - d), nz)],
            send_sem=part_send.at[step, d],
            recv_sem=part_recv.at[step, d],
            device_id=along_z(d, core),
            device_id_type=MESH,
        )

    def share_copy(stage, i, sending):
        d, c = ahead(i // CORES), lax.rem(i, CORES)
        chip, from_core = (z, core) if sending else (lax.rem(z + (nz - d), nz), c)
        return pltpu.make_async_remote_copy(
            src_ref=share.at[stage],
            dst_ref=potential.at[stage, pl.ds(first_block(chip, from_core), piece)],
            send_sem=share_send.at[stage, i],
            recv_sem=share_recv.at[stage, (i - c) + from_core],
            device_id=along_z(d, c),
            device_id_type=MESH,
        )

    def share_mate(stage, sending):
        return pltpu.make_async_remote_copy(
            src_ref=share.at[stage],
            dst_ref=potential.at[stage, pl.ds(first_block(z, core if sending else 1 - core), piece)],
            send_sem=share_send.at[stage, CORES * (OWNERS - 1)],
            recv_sem=share_recv.at[stage, CORES * (OWNERS - 1)],
            device_id=mate,
            device_id_type=MESH,
        )

    def swap_copy(step, spilled):
        return pltpu.make_async_remote_copy(
            src_ref=swap_out.at[step, pl.ds(TILE if spilled else 0, TILE)],
            dst_ref=swap_in.at[step, pl.ds(0 if spilled else TILE, TILE)],
            send_sem=swap_send.at[step, spilled],
            recv_sem=swap_recv.at[step, spilled],
            device_id={"col": left if spilled else right},
            device_id_type=MESH,
        )

    def last_copy(i, sending):
        d = far_first(i, ncol)
        return pltpu.make_async_remote_copy(
            src_ref=last_out,
            dst_ref=last_in.at[pl.ds(TILE * (col if sending else lax.rem(col + (ncol - d), ncol)), TILE)],
            send_sem=last_send.at[d],
            recv_sem=last_recv.at[d],
            device_id={"col": lax.rem(col + d, ncol)},
            device_id_type=MESH,
        )

    def each(count, action):
        def body(i, carry):
            action(i)
            return carry

        lax.fori_loop(0, count, body, 0)

    def iteration(step, carry):
        for spilled in (0, 1):
            for b in range(spilled * homes, (1 + spilled) * homes):
                at = slot_row(b, homes)
                near = [potential[step, pl.ds(table[at, k], 1), :] for k in range(kmax)]
                found = [
                    top_and_total([cost[b * kmax + k, i : i + ROWS, :] + near[k] for k in range(kmax)])
                    for i in range(0, BLOCK, ROWS)
                ]
                top, total = (jnp.transpose(jnp.concatenate(part, axis=0)) for part in zip(*found))
                high = jnp.max(top, axis=0, keepdims=True)
                total = jnp.sum(total * jnp.exp2(top - high), axis=0, keepdims=True)
                swap_out[step, at : at + 1, :] = high + jnp.log2(total)
            if not spilled:

                @pl.when(step == 0)
                def _():
                    pl.semaphore_wait(barrier, greeted)

            swap_copy(step, spilled).start()

        def over_pred(b, carry):
            for k in range(kmax):
                top, total = top_and_total(
                    [
                        cost[b * kmax + k, i : i + TILE, :] + held[lax.rem(b, homes), i : i + TILE, :]
                        for i in range(0, BLOCK, TILE)
                    ]
                )
                high = jnp.max(top, axis=0, keepdims=True)
                tops[b, k : k + 1, :] = high
                sums[b, k : k + 1, :] = jnp.sum(total * jnp.exp2(top - high), axis=0, keepdims=True)
            return carry

        for spilled in (1, 0):
            swap_copy(step, 1 - spilled).wait_recv()
            rows = slice(spilled * TILE, (1 + spilled) * TILE)
            pred_rows = log_a - join(swap_out[step, rows, :], swap_in[step, rows, :])
            if not spilled:

                @pl.when(step == ITERS - 1)
                def _():
                    final = (pred_rows + pred_norm[...]) * (1.0 / UNIT)
                    last_out[...] = final
                    last_in[pl.ds(pl.multiple_of(TILE * col, TILE), TILE), :] = final
                    each(ncol - 1, lambda i: last_copy(i, True).start())

            across = jnp.transpose(jnp.concatenate([pred_rows, jnp.zeros((BLOCK - TILE, BLOCK), F32)], axis=0))
            for b in range(homes):
                held[b] = jnp.broadcast_to(across[:, b : b + 1], (BLOCK, BLOCK))
            lax.fori_loop(spilled * homes, (1 + spilled) * homes, over_pred, 0)

        for b in range(slots):
            value = tops[b] + jnp.log2(sums[b])
            first = value.astype(BF16)
            rest = value - first.astype(F32)
            second = rest.astype(BF16)
            third = (rest - second.astype(F32)).astype(BF16)
            none = jnp.where(iota((LISTS, BLOCK), 0) == 0, NEGATIVE, 0.0).astype(BF16)
            spread[b] = dot(onehot[b], jnp.concatenate([first, second, third, none], axis=0), 0)

        def gather(which):
            for g in range(OWNERS):
                top, total = top_and_total(
                    [spread[b, pl.ds(pl.multiple_of(first_block(g, which), piece), piece), :] for b in range(slots)]
                )
                halves[step, which, g * piece : (g + 1) * piece, :] = top + jnp.log2(total)

        gather(1 - core)
        half_copy(step).start()
        gather(core)
        half_copy(step).wait_recv()
        merged[step] = join(halves[step, core], half_in[step])
        each(nz - 1, lambda i: part_copy(step, i, True).start())
        parts[step, z] = merged[step, pl.ds(pl.multiple_of(lax.rem(z, OWNERS) * piece, piece), piece), :]
        each(nz - 1, lambda i: part_copy(step, nz - 2 - i, False).wait_recv())
        top, total = top_and_total([parts[step, i] for i in range(nz)])
        fresh = log_b - (top + jnp.log2(total))
        own = pl.ds(pl.multiple_of(first_block(z, core), piece), piece)
        fresh = jnp.where(step == ITERS - 1, (fresh + true_norm[own, :]) * (1.0 / UNIT), fresh)
        share[step + 1] = fresh
        potential[step + 1, own, :] = fresh
        each(CORES * (OWNERS - 1), lambda i: share_copy(step + 1, CORES * (OWNERS - 1) - 1 - i, True).start())
        share_mate(step + 1, True).start()

        @pl.when(step == ITERS - 1)
        def _():
            each(ncol - 1, lambda i: last_copy(i, False).wait_recv())

            def place(i, carry):
                pred_out[pl.ds(i, 1), :] = last_in[pl.ds(table[2 * TILE, i], 1), :]
                return carry

            lax.fori_loop(0, pred_out.shape[0], place, 0, unroll=8)
            each(ncol - 1, lambda i: last_copy(i, True).wait_send())

        half_copy(step).wait_send()
        for spilled in (0, 1):
            swap_copy(step, spilled).wait_send()
        each(nz - 1, lambda i: part_copy(step, i, True).wait_send())
        share_mate(step + 1, False).wait_recv()
        each(CORES * (OWNERS - 1), lambda i: share_copy(step + 1, i, False).wait_recv())
        return carry

    lax.fori_loop(0, ITERS, iteration, 0)
    true_out[...] = potential[ITERS, 0:cblocks, :]

    def sent(stage, carry):
        each(CORES * (OWNERS - 1), lambda i: share_copy(stage, i, True).wait_send())
        share_mate(stage, True).wait_send()
        return carry

    lax.fori_loop(1, ITERS + 1, sent, 0)


def on_device(pred_feat, true_feat, neighbors, counts):
    width = pred_feat.shape[1]
    rblocks, cblocks = pred_feat.shape[0] // BLOCK, true_feat.shape[0] // BLOCK
    nrow, ncol = lax.axis_size("row"), lax.axis_size("col")
    nz, homes, kmax = nrow // CORES, rblocks // ncol, neighbors.shape[2]
    slots, half = 2 * homes, cblocks // CORES
    piece = half // OWNERS
    log_a = -math.log2(pred_feat.shape[0] * nrow)
    log_b = -math.log2(true_feat.shape[0] * ncol)
    vmem = pl.BlockSpec(memory_space=pltpu.VMEM)
    hbm = pl.BlockSpec(memory_space=pl.ANY)
    dma = pltpu.SemaphoreType.DMA
    ready = pl.pallas_call(
        functools.partial(prepare_kernel, ncol, homes),
        out_shape=(
            jax.ShapeDtypeStruct((5 * TILE, BLOCK), I32),
            jax.ShapeDtypeStruct((slots, cblocks, 4 * LISTS), BF16),
        ),
        in_specs=[vmem, vmem],
        out_specs=(vmem, vmem),
        compiler_params=pltpu.CompilerParams(vmem_limit_bytes=60 * 2**20),
        name="prepare",
    )(counts.T, jnp.transpose(neighbors, (2, 1, 0)))
    pred_pot, true_pot = pl.pallas_call(
        functools.partial(sinkhorn_kernel, (nz, ncol, homes, kmax, log_a, log_b)),
        out_shape=(
            jax.ShapeDtypeStruct((rblocks, BLOCK), F32),
            jax.ShapeDtypeStruct((cblocks, BLOCK), F32),
        ),
        in_specs=[pl.BlockSpec(memory_space=pltpu.SMEM), hbm, hbm, hbm],
        out_specs=(vmem, vmem),
        scratch_shapes=[
            pltpu.VMEM((width, rblocks * BLOCK), BF16),
            pltpu.VMEM((width, cblocks * BLOCK), BF16),
            pltpu.VMEM((rblocks, width, BLOCK), BF16),
            pltpu.VMEM((cblocks, width, BLOCK), BF16),
            pltpu.VMEM((slots, cblocks, 4 * LISTS), BF16),
            pltpu.VMEM((slots * kmax, BLOCK, BLOCK), F32),
            pltpu.VMEM((TILE, BLOCK), F32),
            pltpu.VMEM((cblocks, BLOCK), F32),
            pltpu.VMEM((ITERS + 1, cblocks + TILE, BLOCK), F32),
            pltpu.VMEM((homes, BLOCK, BLOCK), F32),
            pltpu.VMEM((slots, LISTS, BLOCK), F32),
            pltpu.VMEM((slots, LISTS, BLOCK), F32),
            pltpu.VMEM((slots, cblocks, BLOCK), F32),
            pltpu.VMEM((ITERS, CORES, half, BLOCK), F32),
            pltpu.VMEM((ITERS, half, BLOCK), F32),
            pltpu.VMEM((ITERS, half, BLOCK), F32),
            pltpu.VMEM((ITERS, nz, piece, BLOCK), F32),
            pltpu.VMEM((ITERS + 1, piece, BLOCK), F32),
            pltpu.VMEM((ITERS, 2 * TILE, BLOCK), F32),
            pltpu.VMEM((ITERS, 2 * TILE, BLOCK), F32),
            pltpu.VMEM((TILE, BLOCK), F32),
            pltpu.VMEM((TILE * ncol, BLOCK), F32),
            dma((3,)),
            dma((ITERS,)),
            dma((ITERS,)),
            dma((ITERS, nz)),
            dma((ITERS, nz)),
            dma((ITERS + 1, CORES * (OWNERS - 1) + 1)),
            dma((ITERS + 1, CORES * (OWNERS - 1) + 1)),
            dma((ITERS, 2)),
            dma((ITERS, 2)),
            dma((ncol,)),
            dma((ncol,)),
        ],
        compiler_params=pltpu.CompilerParams(
            collective_id=0, has_side_effects=True, vmem_limit_bytes=60 * 2**20
        ),
        name="sinkhorn",
    )(*ready, pred_feat.T, true_feat.T)
    return (pred_pot.reshape(-1), true_pot.reshape(-1))


def solution(mesh):
    in_specs = (P("row", None), P("col", None), P("row", "col", None), P("row", None))
    out_specs = (P("row"), P("col"))
    return jax.shard_map(
        on_device, mesh=mesh, in_specs=in_specs, out_specs=out_specs, check_vma=False
    )
```

```python
import functools
import math

import jax
import jax.numpy as jnp
from jax import lax
from jax.experimental import pallas as pl
from jax.experimental.pallas import tpu as pltpu
from jax.sharding import PartitionSpec as P

BLOCK = 128
ITERS = 3
EPSILON = 0.02
NEGATIVE = -1e30
TILE = 8
CORES = 2
ROWS = 16
OWNERS = 4
LISTS = 16
PICK_LANE = 63
UNIT = 1.0 / (EPSILON * math.log(2.0))
MESH = pl.DeviceIdType.MESH
F32, BF16, I32 = jnp.float32, jnp.bfloat16, jnp.int32


def dot(a, b, b_axis):
    return lax.dot_general(a, b, (((1,), (b_axis,)), ((), ())), preferred_element_type=F32)


def iota(shape, axis):
    return lax.broadcasted_iota(I32, shape, axis)


def join(a, b):
    high, low = jnp.maximum(a, b), jnp.minimum(a, b)
    return high + jnp.log2(1.0 + jnp.exp2(low - high))


def tree(op, items):
    items = list(items)
    while len(items) > 1:
        items = [op(*items[i : i + 2]) if i + 1 < len(items) else items[i] for i in range(0, len(items), 2)]
    return items[0]


def top_and_total(items):
    top = tree(jnp.maximum, items)
    return top, tree(jnp.add, [jnp.exp2(item - top) for item in items])


def square_norms(block):
    wide = block.astype(F32)
    return jnp.sum(wide * wide, axis=0, keepdims=True)


def slot_row(b, homes):
    return b if b < homes else b + (TILE - homes)


def prepare_kernel(ncol, homes, counts_ref, neighbors_ref, table_ref, onehot):
    here = lax.axis_index("col")
    cblocks = onehot.shape[1]
    counts = counts_ref[...].astype(F32)
    blocks, kmax = counts.shape[1], neighbors_ref.shape[0]
    to, frm = iota((ncol, ncol), 0), iota((ncol, ncol), 1)
    before = (frm == lax.rem(to + (ncol - 1), ncol)).astype(F32)
    home = ((counts > 0.5) & (dot(before, counts, 0) < 0.5)).astype(F32)
    upto = (iota((blocks, blocks), 0) <= iota((blocks, blocks), 1)).astype(F32)
    rank = dot(home, upto, 0) - 1.0
    shard = iota(home.shape, 0).astype(F32)
    place = jnp.sum(home * (TILE * shard + rank), axis=0, keepdims=True)
    slot = iota((2 * TILE, blocks), 0)
    owner = jnp.where(slot < TILE, here, lax.rem(here + (ncol - 1), ncol))
    wanted = (TILE * owner + lax.rem(slot, TILE)).astype(F32)
    chosen = (place == wanted).astype(F32)
    count = jnp.sum(jnp.where(iota(counts.shape, 0) == here, counts, 0.0), axis=0, keepdims=True)
    count = jnp.sum(chosen * count, axis=1, keepdims=True)
    pick = jnp.sum(chosen * iota(chosen.shape, 1).astype(F32), axis=1, keepdims=True)
    lane = iota((kmax, BLOCK), 1)
    repeat = ((lax.rem(lane, LISTS) == iota((kmax, BLOCK), 0)) & (lane < 3 * LISTS)).astype(F32)
    listed = dot(dot(chosen, neighbors_ref[:, 0, :].astype(F32), 1), repeat, 0)
    lane = iota(listed.shape, 1)
    live = lax.rem(lane, LISTS).astype(F32) < count
    found = jnp.where(lane == PICK_LANE, pick, jnp.where(live, listed, float(cblocks)))
    table_ref[0 : 2 * TILE, :] = found.astype(I32)
    table_ref[2 * TILE : 3 * TILE, :] = jnp.zeros((TILE, BLOCK), I32)
    table_ref[2 * TILE : 2 * TILE + 1, 0:blocks] = place.astype(I32)
    first_named = jnp.where(lane == PICK_LANE, pick, jnp.where(live, listed, 0.0))
    table_ref[3 * TILE : 5 * TILE, :] = first_named.astype(I32)

    for b in range(2 * homes):
        at = slot_row(b, homes)
        listed = table_ref[at : at + 1, 0 : 4 * LISTS]
        lane = iota((cblocks, 4 * LISTS), 1)
        match = ((iota((cblocks, 4 * LISTS), 0) == listed) & (lane < 3 * LISTS)).astype(F32)
        absent = 1.0 - jnp.sum(jnp.where(lane < LISTS, match, 0.0), axis=1, keepdims=True)
        onehot[b] = jnp.where(lane == 3 * LISTS, absent, match).astype(BF16)


def sinkhorn_kernel(
    sizes, table, onehot_hbm, pred_hbm, true_hbm, pred_out, true_out,
    pred, true, pred_blocks, true_blocks, onehot, cost, pred_norm, true_norm,
    potential, held, tops, sums, spread,
    halves, half_in, merged, parts, share, swap_out, swap_in, last_out, last_in,
    load_sem, half_send, half_recv, part_send, part_recv, share_send, share_recv, swap_send, swap_recv, last_send, last_recv,
):
    nz, ncol, homes, kmax, log_a, log_b = sizes
    row, col = lax.axis_index("row"), lax.axis_index("col")
    z, core = row // CORES, lax.rem(row, CORES)
    slots = 2 * homes
    cblocks, width = true_norm.shape[0], true.shape[0]
    right, left = lax.rem(col + 1, ncol), lax.rem(col + (ncol - 1), ncol)
    mate = {"row": z * CORES + (1 - core)}
    piece = cblocks // (OWNERS * CORES)
    half = OWNERS * piece

    def far_first(i, n):
        return n // 2 + (1 - 2 * lax.rem(i, 2)) * ((i + 1) // 2)

    def along_z(d, c):
        return {"row": lax.rem(z + d, nz) * CORES + c}

    def ahead(i):
        return jnp.where(i == 0, 1, nz - i)

    def first_block(chip, c):
        return lax.rem(chip, OWNERS) * (CORES * piece) + c * piece

    loads = [
        pltpu.make_async_copy(true_hbm, true, load_sem.at[0]),
        pltpu.make_async_copy(pred_hbm, pred, load_sem.at[1]),
        pltpu.make_async_copy(onehot_hbm, onehot, load_sem.at[2]),
    ]
    for load in loads:
        load.start()

    barrier = pltpu.get_barrier_semaphore()

    def greet(device):
        pl.semaphore_signal(barrier, inc=1, device_id=device, device_id_type=MESH)

    def greet_z(i, carry):
        greet(along_z(i, core))
        return carry

    def greet_col(i, carry):
        greet({"col": lax.rem(col + i, ncol)})
        return carry

    lax.fori_loop(1, nz, greet_z, 0)
    lax.fori_loop(1, ncol, greet_col, 0)
    near = sorted({d % nz for d in (1, -1, 2, -2)})
    for d in near:
        greet(along_z(d, 1 - core))
    greet(mate)
    greeted = nz - 1 + ncol - 1 + len(near) + 1

    for step in range(ITERS):
        potential[step, cblocks : cblocks + TILE, :] = jnp.full((TILE, BLOCK), NEGATIVE, F32)
    swap_out[...] = jnp.zeros(swap_out.shape, F32)
    tops[...] = jnp.zeros(tops.shape, F32)
    sums[...] = jnp.ones(sums.shape, F32)
    pred_norm[...] = jnp.zeros(pred_norm.shape, F32)
    loads[0].wait()

    def take_true(i, carry):
        block = true[:, pl.ds(pl.multiple_of(BLOCK * i, BLOCK), BLOCK)]
        true_blocks[i] = block
        true_norm[pl.ds(i, 1), :] = square_norms(block) * (UNIT / width)
        return carry

    lax.fori_loop(0, cblocks, take_true, 0, unroll=16)
    potential[0, 0:cblocks, :] = -true_norm[...]
    loads[1].wait()

    def take_pred(i, carry):
        pred_blocks[i] = pred[:, pl.ds(pl.multiple_of(BLOCK * i, BLOCK), BLOCK)]
        return carry

    lax.fori_loop(0, pred_out.shape[0], take_pred, 0, unroll=16)
    loads[2].wait()
    for b in range(homes):
        pred_norm[b : b + 1, :] = square_norms(pred_blocks[table[b, PICK_LANE]]) * (UNIT / width)

    def products(b, carry):
        at = 3 * TILE + jnp.where(b < homes, b, b + (TILE - homes))
        mine = jnp.transpose(pred_blocks[table[at, PICK_LANE]])
        for k in range(kmax):
            cost[b * kmax + k] = dot(mine, true_blocks[table[at, k]], 0) * (2.0 * UNIT / width)
        return carry

    lax.fori_loop(0, slots, products, 0)

    def half_copy(step):
        return pltpu.make_async_remote_copy(
            src_ref=halves.at[step, 1 - core],
            dst_ref=half_in.at[step],
            send_sem=half_send.at[step],
            recv_sem=half_recv.at[step],
            device_id=mate,
            device_id_type=MESH,
        )

    def part_copy(step, i, sending):
        d = far_first(i, nz)
        return pltpu.make_async_remote_copy(
            src_ref=merged.at[step, pl.ds(lax.rem(lax.rem(z + d, nz), OWNERS) * piece, piece)],
            dst_ref=parts.at[step, z if sending else lax.rem(z + (nz - d), nz)],
            send_sem=part_send.at[step, d],
            recv_sem=part_recv.at[step, d],
            device_id=along_z(d, core),
            device_id_type=MESH,
        )

    def share_copy(stage, i, sending):
        d, c = ahead(i // CORES), lax.rem(i, CORES)
        chip, from_core = (z, core) if sending else (lax.rem(z + (nz - d), nz), c)
        return pltpu.make_async_remote_copy(
            src_ref=share.at[stage],
            dst_ref=potential.at[stage, pl.ds(first_block(chip, from_core), piece)],
            send_sem=share_send.at[stage, i],
            recv_sem=share_recv.at[stage, (i - c) + from_core],
            device_id=along_z(d, c),
            device_id_type=MESH,
        )

    def share_mate(stage, sending):
        return pltpu.make_async_remote_copy(
            src_ref=share.at[stage],
            dst_ref=potential.at[stage, pl.ds(first_block(z, core if sending else 1 - core), piece)],
            send_sem=share_send.at[stage, CORES * (OWNERS - 1)],
            recv_sem=share_recv.at[stage, CORES * (OWNERS - 1)],
            device_id=mate,
            device_id_type=MESH,
        )

    def swap_copy(step, spilled):
        return pltpu.make_async_remote_copy(
            src_ref=swap_out.at[step, pl.ds(TILE if spilled else 0, TILE)],
            dst_ref=swap_in.at[step, pl.ds(0 if spilled else TILE, TILE)],
            send_sem=swap_send.at[step, spilled],
            recv_sem=swap_recv.at[step, spilled],
            device_id={"col": left if spilled else right},
            device_id_type=MESH,
        )

    def last_copy(i, sending):
        d = far_first(i, ncol)
        return pltpu.make_async_remote_copy(
            src_ref=last_out,
            dst_ref=last_in.at[pl.ds(TILE * (col if sending else lax.rem(col + (ncol - d), ncol)), TILE)],
            send_sem=last_send.at[d],
            recv_sem=last_recv.at[d],
            device_id={"col": lax.rem(col + d, ncol)},
            device_id_type=MESH,
        )

    def each(count, action):
        def body(i, carry):
            action(i)
            return carry

        lax.fori_loop(0, count, body, 0)

    def iteration(step, carry):
        for spilled in (0, 1):
            for b in range(spilled * homes, (1 + spilled) * homes):
                at = slot_row(b, homes)
                near = [potential[step, pl.ds(table[at, k], 1), :] for k in range(kmax)]
                found = [
                    top_and_total([cost[b * kmax + k, i : i + ROWS, :] + near[k] for k in range(kmax)])
                    for i in range(0, BLOCK, ROWS)
                ]
                top, total = (jnp.transpose(jnp.concatenate(part, axis=0)) for part in zip(*found))
                high = jnp.max(top, axis=0, keepdims=True)
                total = jnp.sum(total * jnp.exp2(top - high), axis=0, keepdims=True)
                swap_out[step, at : at + 1, :] = high + jnp.log2(total)
            if not spilled:

                @pl.when(step == 0)
                def _():
                    pl.semaphore_wait(barrier, greeted)

            swap_copy(step, spilled).start()

        def over_pred(b, carry):
            for k in range(kmax):
                top, total = top_and_total(
                    [
                        cost[b * kmax + k, i : i + TILE, :] + held[lax.rem(b, homes), i : i + TILE, :]
                        for i in range(0, BLOCK, TILE)
                    ]
                )
                high = jnp.max(top, axis=0, keepdims=True)
                tops[b, k : k + 1, :] = high
                sums[b, k : k + 1, :] = jnp.sum(total * jnp.exp2(top - high), axis=0, keepdims=True)
            return carry

        for spilled in (1, 0):
            swap_copy(step, 1 - spilled).wait_recv()
            rows = slice(spilled * TILE, (1 + spilled) * TILE)
            pred_rows = log_a - join(swap_out[step, rows, :], swap_in[step, rows, :])
            if not spilled:

                @pl.when(step == ITERS - 1)
                def _():
                    final = (pred_rows + pred_norm[...]) * (1.0 / UNIT)
                    last_out[...] = final
                    last_in[pl.ds(pl.multiple_of(TILE * col, TILE), TILE), :] = final
                    each(ncol - 1, lambda i: last_copy(i, True).start())

            across = jnp.transpose(jnp.concatenate([pred_rows, jnp.zeros((BLOCK - TILE, BLOCK), F32)], axis=0))
            for b in range(homes):
                held[b] = jnp.broadcast_to(across[:, b : b + 1], (BLOCK, BLOCK))
            lax.fori_loop(spilled * homes, (1 + spilled) * homes, over_pred, 0)

        for b in range(slots):
            value = tops[b] + jnp.log2(sums[b])
            first = value.astype(BF16)
            rest = value - first.astype(F32)
            second = rest.astype(BF16)
            third = (rest - second.astype(F32)).astype(BF16)
            none = jnp.where(iota((LISTS, BLOCK), 0) == 0, NEGATIVE, 0.0).astype(BF16)
            spread[b] = dot(onehot[b], jnp.concatenate([first, second, third, none], axis=0), 0)

        def gather(which):
            for g in range(OWNERS):
                top, total = top_and_total(
                    [spread[b, pl.ds(pl.multiple_of(first_block(g, which), piece), piece), :] for b in range(slots)]
                )
                halves[step, which, g * piece : (g + 1) * piece, :] = top + jnp.log2(total)

        gather(1 - core)
        half_copy(step).start()
        gather(core)
        half_copy(step).wait_recv()
        merged[step] = join(halves[step, core], half_in[step])
        each(nz - 1, lambda i: part_copy(step, i, True).start())
        parts[step, z] = merged[step, pl.ds(pl.multiple_of(lax.rem(z, OWNERS) * piece, piece), piece), :]
        each(nz - 1, lambda i: part_copy(step, nz - 2 - i, False).wait_recv())
        top, total = top_and_total([parts[step, i] for i in range(nz)])
        fresh = log_b - (top + jnp.log2(total))
        own = pl.ds(pl.multiple_of(first_block(z, core), piece), piece)
        fresh = jnp.where(step == ITERS - 1, (fresh + true_norm[own, :]) * (1.0 / UNIT), fresh)
        share[step + 1] = fresh
        potential[step + 1, own, :] = fresh
        each(CORES * (OWNERS - 1), lambda i: share_copy(step + 1, CORES * (OWNERS - 1) - 1 - i, True).start())
        share_mate(step + 1, True).start()

        @pl.when(step == ITERS - 1)
        def _():
            each(ncol - 1, lambda i: last_copy(i, False).wait_recv())

            def place(i, carry):
                pred_out[pl.ds(i, 1), :] = last_in[pl.ds(table[2 * TILE, i], 1), :]
                return carry

            lax.fori_loop(0, pred_out.shape[0], place, 0, unroll=8)
            each(ncol - 1, lambda i: last_copy(i, True).wait_send())

        half_copy(step).wait_send()
        for spilled in (0, 1):
            swap_copy(step, spilled).wait_send()
        each(nz - 1, lambda i: part_copy(step, i, True).wait_send())
        share_mate(step + 1, False).wait_recv()
        each(CORES * (OWNERS - 1), lambda i: share_copy(step + 1, i, False).wait_recv())
        return carry

    lax.fori_loop(0, ITERS, iteration, 0)
    true_out[...] = potential[ITERS, 0:cblocks, :]

    def sent(stage, carry):
        each(CORES * (OWNERS - 1), lambda i: share_copy(stage, i, True).wait_send())
        share_mate(stage, True).wait_send()
        return carry

    lax.fori_loop(1, ITERS + 1, sent, 0)


def on_device(pred_feat, true_feat, neighbors, counts):
    width = pred_feat.shape[1]
    rblocks, cblocks = pred_feat.shape[0] // BLOCK, true_feat.shape[0] // BLOCK
    nrow, ncol = lax.axis_size("row"), lax.axis_size("col")
    nz, homes, kmax = nrow // CORES, rblocks // ncol, neighbors.shape[2]
    slots, half = 2 * homes, cblocks // CORES
    piece = half // OWNERS
    log_a = -math.log2(pred_feat.shape[0] * nrow)
    log_b = -math.log2(true_feat.shape[0] * ncol)
    vmem = pl.BlockSpec(memory_space=pltpu.VMEM)
    hbm = pl.BlockSpec(memory_space=pl.ANY)
    dma = pltpu.SemaphoreType.DMA
    ready = pl.pallas_call(
        functools.partial(prepare_kernel, ncol, homes),
        out_shape=(
            jax.ShapeDtypeStruct((5 * TILE, BLOCK), I32),
            jax.ShapeDtypeStruct((slots, cblocks, 4 * LISTS), BF16),
        ),
        in_specs=[vmem, vmem],
        out_specs=(vmem, vmem),
        compiler_params=pltpu.CompilerParams(vmem_limit_bytes=53 * 2**20),
        name="prepare",
    )(counts.T, jnp.transpose(neighbors, (2, 1, 0)))
    pred_pot, true_pot = pl.pallas_call(
        functools.partial(sinkhorn_kernel, (nz, ncol, homes, kmax, log_a, log_b)),
        out_shape=(
            jax.ShapeDtypeStruct((rblocks, BLOCK), F32),
            jax.ShapeDtypeStruct((cblocks, BLOCK), F32),
        ),
        in_specs=[pl.BlockSpec(memory_space=pltpu.SMEM), hbm, hbm, hbm],
        out_specs=(vmem, vmem),
        scratch_shapes=[
            pltpu.VMEM((width, rblocks * BLOCK), BF16),
            pltpu.VMEM((width, cblocks * BLOCK), BF16),
            pltpu.VMEM((rblocks, width, BLOCK), BF16),
            pltpu.VMEM((cblocks, width, BLOCK), BF16),
            pltpu.VMEM((slots, cblocks, 4 * LISTS), BF16),
            pltpu.VMEM((slots * kmax, BLOCK, BLOCK), F32),
            pltpu.VMEM((TILE, BLOCK), F32),
            pltpu.VMEM((cblocks, BLOCK), F32),
            pltpu.VMEM((ITERS + 1, cblocks + TILE, BLOCK), F32),
            pltpu.VMEM((homes, BLOCK, BLOCK), F32),
            pltpu.VMEM((slots, LISTS, BLOCK), F32),
            pltpu.VMEM((slots, LISTS, BLOCK), F32),
            pltpu.VMEM((slots, cblocks, BLOCK), F32),
            pltpu.VMEM((ITERS, CORES, half, BLOCK), F32),
            pltpu.VMEM((ITERS, half, BLOCK), F32),
            pltpu.VMEM((ITERS, half, BLOCK), F32),
            pltpu.VMEM((ITERS, nz, piece, BLOCK), F32),
            pltpu.VMEM((ITERS + 1, piece, BLOCK), F32),
            pltpu.VMEM((ITERS, 2 * TILE, BLOCK), F32),
            pltpu.VMEM((ITERS, 2 * TILE, BLOCK), F32),
            pltpu.VMEM((TILE, BLOCK), F32),
            pltpu.VMEM((TILE * ncol, BLOCK), F32),
            dma((3,)),
            dma((ITERS,)),
            dma((ITERS,)),
            dma((ITERS, nz)),
            dma((ITERS, nz)),
            dma((ITERS + 1, CORES * (OWNERS - 1) + 1)),
            dma((ITERS + 1, CORES * (OWNERS - 1) + 1)),
            dma((ITERS, 2)),
            dma((ITERS, 2)),
            dma((ncol,)),
            dma((ncol,)),
        ],
        compiler_params=pltpu.CompilerParams(
            collective_id=0, has_side_effects=True, vmem_limit_bytes=53 * 2**20
        ),
        name="sinkhorn",
    )(*ready, pred_feat.T, true_feat.T)
    return (pred_pot.reshape(-1), true_pot.reshape(-1))


def solution(mesh):
    in_specs = (P("row", None), P("col", None), P("row", "col", None), P("row", None))
    out_specs = (P("row"), P("col"))
    return jax.shard_map(
        on_device, mesh=mesh, in_specs=in_specs, out_specs=out_specs, check_vma=False
    )
```
